512 devices in a mesh: rep: 16 (over z_hi, y), seq: 32 (over z_lo, x, core).
Axes of the slice: x: 4, y: 4, z: 16 (z_hi: 4, z_lo: 4; z = z_hi * 4 + z_lo), core: 2. Of those that a mesh axis runs over, the one named last changes fastest.
Arguments:
- qkv_spatial: bfloat16 [131072, 1728], P(('rep', 'seq')), may hold values from -5.5 to 5.5
- qkv_temporal: bfloat16 [131072, 1728], P(('rep', 'seq')), may hold values from -5.5 to 5.5
- out_grad: bfloat16 [131072, 1152], P(('rep', 'seq')), may hold values from -6 to 6
- out_proj: bfloat16 [576, 2, 1152], P('seq'), may hold values from -0.25 to 0.25
Outputs:
- qkv_spatial_grad: bfloat16 [131072, 1728], P(('rep', 'seq'))
- qkv_temporal_grad: bfloat16 [131072, 1728], P(('rep', 'seq'))
- out_proj_grad: bfloat16 [576, 2, 1152], P('seq')
The draws below stay inside these ranges and needn't reach their ends.
All inputs are finite; a program needn't handle non-finite values.
Results may differ from the reference program's by a relative error of at most 0.015.
Values may be sent and summed in bfloat16 or wider, within the bound.
A program may use at most 128 MiB of HBM per device.

```python
import jax
import jax.numpy as jnp
from jax import lax

D = 1152
HEADS = 8
HEAD_DIM = 72
PATCHES = 256
INNER = 576
FRAMES = 32
TOKENS = 131072
N_REP = 16


def sample_fields(key, portion, lowest, highest):
    streams = jax.random.split(key, 4)
    normal_part = jnp.clip(jax.random.normal(streams[0], (TOKENS, 3, HEADS, HEAD_DIM), jnp.float32), -4.0, 4.0)
    direction = jnp.where(jax.random.bernoulli(streams[1], 0.5, (HEADS, HEAD_DIM)), 1.0, -1.0)
    chosen = jax.random.uniform(streams[2], (TOKENS, 2, 1, 1)) < portion
    strength = jax.random.uniform(streams[3], (TOKENS, 2, 1, 1), minval=lowest, maxval=highest)
    aligned = strength * direction
    query_key = jnp.where(chosen, aligned, normal_part[:, :2])
    fields = jnp.concatenate([query_key, normal_part[:, 2:]], axis=1)
    return fields.reshape(TOKENS, 3 * HEADS * HEAD_DIM).astype(jnp.bfloat16)


def draw_qkv_spatial(key, part):
    key = jax.random.fold_in(key, 1)
    return sample_fields(key, 0.0, 0.0, 0.0)


def draw_qkv_temporal(key, part):
    key = jax.random.fold_in(key, 2)
    return sample_fields(key, 0.0, 0.0, 0.0)


def levels(own_key, dims, shards, smallest, top_value):
    level, own = 1.0, jax.random.fold_in(own_key, 6)
    for position, parts in shards:
        draws = jnp.exp(jax.random.uniform(jax.random.fold_in(own, position), (parts,), jnp.float32, smallest / len(shards), top_value / len(shards)))
        level = level * jnp.repeat(draws, dims[position] // parts).reshape([-1 if axis == position else 1 for axis in range(len(dims))])
    return level


def gaussian(key, dims, width, most, shards=(), held_as=jnp.bfloat16):
    factor_of = levels(key, dims, shards, -0.22, 0.18) if shards else 1.0
    result = jax.random.normal(key, dims, jnp.float32) * width * factor_of
    return jnp.minimum(jnp.maximum(result, -most), most).astype(held_as)


def setup_inputs(seed: int = 0) -> dict:
    arg_keys = jax.random.split(jax.random.key(seed), 5)
    return {
        "qkv_spatial": draw_qkv_spatial(jax.random.fold_in(arg_keys[4], 71), 0),
        "qkv_temporal": draw_qkv_temporal(jax.random.fold_in(arg_keys[4], 71), 0),
        "out_grad": gaussian(arg_keys[2], (TOKENS, D), 1.0, 6.0, ((0, 512),)),
        "out_proj": gaussian(arg_keys[3], (INNER, 2, D), INNER ** -0.5, 0.25, ((0, 32),)),
    }


def product(layout, left, right):
    return jnp.einsum(layout, left.astype(jnp.float32), right.astype(jnp.float32), precision=lax.Precision.HIGHEST)


def attend(query, keys, values):
    scaling = query.shape[-1] ** -0.5
    scores = product("glhe,gmhe->ghlm", query, keys) * scaling
    highest = jnp.max(scores, axis=-1, keepdims=True)
    weights = jnp.exp(scores - highest)
    probs = weights / jnp.sum(weights, axis=-1, keepdims=True)
    mixed = product("ghlm,gmhe->glhe", probs.astype(jnp.bfloat16), values).astype(jnp.bfloat16)
    return mixed, probs


def attend_back(query, keys, values, probs, grad_mixed):
    scaling = query.shape[-1] ** -0.5
    rounded = probs.astype(jnp.bfloat16)
    grad_values = product("ghlm,glhe->gmhe", rounded, grad_mixed)
    grad_probs = product("glhe,gmhe->ghlm", grad_mixed, values)
    grad_scores = (probs * (grad_probs - jnp.sum(grad_probs * probs, axis=-1, keepdims=True))).astype(jnp.bfloat16)
    grad_query = product("ghlm,gmhe->glhe", grad_scores, keys) * scaling
    grad_keys = product("ghlm,glhe->gmhe", grad_scores, query) * scaling
    return grad_query, grad_keys, grad_values


def reference(qkv_spatial, qkv_temporal, out_grad, out_proj):
    inner_width = HEADS * HEAD_DIM
    factor = float(TOKENS) ** -0.5
    weights = out_proj.astype(jnp.float32)
    spatial_all = qkv_spatial.reshape(N_REP, FRAMES, PATCHES, 3, HEADS, HEAD_DIM)
    temporal_all = qkv_temporal.reshape(N_REP, FRAMES, PATCHES, 3, HEADS, HEAD_DIM)
    cotangent_all = out_grad.reshape(N_REP, FRAMES, PATCHES, D)

    def one_video(inputs_video):
        spatial, temporal, cotangent = inputs_video
        spatial_mixed, spatial_probs = attend(spatial[:, :, 0], spatial[:, :, 1], spatial[:, :, 2])
        spatial_grad = product("fpd,nd->fpn", cotangent, weights[:, 0]).astype(jnp.bfloat16)
        spatial_grad = spatial_grad.reshape(FRAMES, PATCHES, HEADS, HEAD_DIM)
        spatial_back = attend_back(spatial[:, :, 0], spatial[:, :, 1], spatial[:, :, 2], spatial_probs, spatial_grad)
        spatial_fields = jnp.stack(spatial_back, axis=2).astype(jnp.bfloat16).reshape(FRAMES, PATCHES, 3 * inner_width)
        temporal_in = jnp.transpose(temporal, (1, 0, 2, 3, 4))
        temporal_cot = jnp.transpose(cotangent, (1, 0, 2))
        temporal_mixed, temporal_probs = attend(temporal_in[:, :, 0], temporal_in[:, :, 1], temporal_in[:, :, 2])
        temporal_grad = product("pfd,nd->pfn", temporal_cot, weights[:, 1]).astype(jnp.bfloat16)
        temporal_grad = temporal_grad.reshape(PATCHES, FRAMES, HEADS, HEAD_DIM)
        temporal_back = attend_back(temporal_in[:, :, 0], temporal_in[:, :, 1], temporal_in[:, :, 2], temporal_probs, temporal_grad)
        temporal_fields = jnp.stack(temporal_back, axis=2).astype(jnp.bfloat16)
        temporal_fields = jnp.transpose(temporal_fields, (1, 0, 2, 3, 4)).reshape(FRAMES, PATCHES, 3 * inner_width)
        cotangent_rows = cotangent.reshape(FRAMES * PATCHES, D)
        spatial_rows = spatial_mixed.reshape(FRAMES * PATCHES, inner_width)
        spatial_weight = product("nh,nd->hd", spatial_rows, cotangent_rows) * factor
        temporal_frames = jnp.transpose(temporal_mixed, (1, 0, 2, 3)).reshape(FRAMES * PATCHES, inner_width)
        temporal_weight = product("nh,nd->hd", temporal_frames, cotangent_rows) * factor
        return spatial_fields, temporal_fields, spatial_weight, temporal_weight

    spatial_fields, temporal_fields, spatial_weight, temporal_weight = lax.map(one_video, (spatial_all, temporal_all, cotangent_all))
    proj_grad = jnp.stack([jnp.sum(spatial_weight, axis=0), jnp.sum(temporal_weight, axis=0)], axis=1).astype(jnp.bfloat16)
    return spatial_fields.reshape(TOKENS, 3 * inner_width), temporal_fields.reshape(TOKENS, 3 * inner_width), proj_grad
```

```python
import functools

import jax
import jax.numpy as jnp
from jax import lax
from jax.experimental import pallas as pl
from jax.experimental.pallas import tpu as pltpu
from jax.sharding import PartitionSpec as P

HEADS, HEAD_DIM, PATCHES, FRAMES = 8, 72, 256, 32
INNER, WIDTH, D = 576, 1728, 1152
PAD = 640
GROUP = 8
ROWS = 18
BLOCK = 24
HALF = 16 * BLOCK
SEQ, TOKENS = 32, 131072
SCALING = HEAD_DIM**-0.5
FACTOR = float(TOKENS) ** -0.5
F32, BF16 = jnp.float32, jnp.bfloat16


def dot(left, right, dims=((1,), (0,))):
    return lax.dot_general(left, right, (dims, ((), ())), preferred_element_type=F32)


def kernel(
    qkvs_ref, qkvt_ref, og_ref, w_ref,
    gs_ref, gt_ref, gw_ref,
    qkvs, og2, qtr, das, dar, mts, mtr, gts, wbuf, wf, wmat, sel, self32, dah, dax, m2, mx,
    gbuf, yrecv, xbuf, xrecv, zbuf, zrecv, z2buf, z2recv, res,
    qs, ks, vs, ds, qt, kt, vt, dt, probs_s, probs_t, acc0, acc1, acc2, gstage,
    lsem, wz_s, wz_r, wx_s, wx_r, og_s, og_r, a_s, a_r, b_s, b_r, c_s, c_r, d_s, d_r,
    p_s, p_r, y_s, y_r, x_s, x_r, z_s, z_r, zz_s, zz_r, f_s, f_r,
):
    rep, me = lax.axis_index("rep"), lax.axis_index("seq")
    zh, y = rep // 4, lax.rem(rep, 4)
    zl, x, core = me // 8, lax.rem(me // 2, 4), lax.rem(me, 2)
    z = 4 * zh + zl

    def at(rep_to, seq_to):
        return {"device_id": (rep_to, seq_to), "device_id_type": pl.DeviceIdType.MESH}

    def at_z(step):
        to = lax.rem(z + step + 16, 16)
        return at((to // 4) * 4 + y, lax.rem(to, 4) * 8 + lax.rem(me, 8))

    def at_y(step):
        return at(zh * 4 + lax.rem(y + step, 4), me)

    def at_zh(step):
        return at(lax.rem(zh + step, 4) * 4 + y, me)

    def at_x(step):
        return at(rep, zl * 8 + lax.rem(x + step, 4) * 2 + core)

    partner = at(rep, me + 1 - 2 * core)

    def remote(src, dst, send, recv, target):
        return pltpu.make_async_remote_copy(
            src_ref=src, dst_ref=dst, send_sem=send, recv_sem=recv, **target
        )

    barrier = pltpu.get_barrier_semaphore()

    def greet(k, carry):
        pl.semaphore_signal(barrier, inc=1, **at(rep, lax.rem(me + k, SEQ)))
        return carry

    lax.fori_loop(1, SEQ, greet, 0)
    for step in (-1, -2, 1):
        pl.semaphore_signal(barrier, inc=1, **at_z(step))
    for step in (1, 2, 3):
        pl.semaphore_signal(barrier, inc=1, **at_y(step))
        pl.semaphore_signal(barrier, inc=1, **at_zh(step))

    local = [
        pltpu.make_async_copy(qkvs_ref, qkvs, lsem.at[0]),
        pltpu.make_async_copy(og_ref, og2.at[pl.ds(0, PATCHES)], lsem.at[1]),
        pltpu.make_async_copy(qkvt_ref.at[me], qtr.at[me], lsem.at[2]),
        pltpu.make_async_copy(w_ref.at[0], wbuf.at[0, x, zl], lsem.at[3]),
        pltpu.make_async_copy(w_ref.at[1], wbuf.at[1, x, zl], lsem.at[4]),
    ]
    for copy in local:
        copy.start()

    pl.semaphore_wait(barrier, 31 + 9)

    wz = [
        [
            remote(w_ref.at[b], wbuf.at[b, x, zl], wz_s.at[b, i], wz_r.at[b, i], at_z(step))
            for i, step in enumerate((1, 2, -1))
        ]
        for b in (0, 1)
    ]
    for copy in wz[1] + wz[0]:
        copy.start()
    og_copy = remote(
        og_ref, og2.at[pl.ds(PATCHES, PATCHES)], og_s.at[0], og_r.at[0], partner
    )
    og_copy.start()

    def exchange(src, dst, send, recv):
        def copy(k):
            to = lax.rem(me + k, SEQ)
            return remote(src.at[to], dst.at[me], send.at[k], recv.at[k], at(rep, to))

        def start(k, carry):
            copy(k).start()
            return carry

        def landed(k, carry):
            copy(k).wait_recv()
            return carry

        def sent(k, carry):
            copy(k).wait_send()
            return carry

        return (
            lambda: lax.fori_loop(1, SEQ, start, 0),
            lambda: lax.fori_loop(1, SEQ, landed, 0),
            lambda: lax.fori_loop(1, SEQ, sent, 0),
        )

    fields_out = exchange(qkvt_ref, qtr, a_s, a_r)
    grads_out = exchange(das, dar, b_s, b_r)
    mixed_back = exchange(mts, mtr, c_s, c_r)
    fields_back = exchange(gts, gt_ref, d_s, d_r)
    fields_out[0]()

    def fill_sel(i, carry):
        xx, zz = i // 4, lax.rem(i, 4)
        j = lax.broadcasted_iota(jnp.int32, (BLOCK, PAD), 0)
        n = lax.broadcasted_iota(jnp.int32, (BLOCK, PAD), 1)
        rows = pl.ds(pl.multiple_of(i * BLOCK, BLOCK), BLOCK)
        for which in (0, 1):
            parity = core if which == 0 else 1 - core
            first = ROWS * (8 * zz + 2 * xx + parity)
            hit = (n == first + j) & (j < ROWS)
            self32[which, rows, :] = jnp.where(hit, 1.0, 0.0)
        return carry

    lax.fori_loop(0, 16, fill_sel, 0)
    for which in (0, 1):
        sel[which] = self32[which].astype(BF16)
    wf[...] = jnp.zeros_like(wf)

    def split(fields, q, k, v):
        q[...] = fields[:, 0:PAD].astype(BF16)
        k[...] = pltpu.roll(fields[:, 512:1152], PAD - 64, 1).astype(BF16)
        v[:, 512:PAD] = jnp.zeros((PATCHES, PAD - 512), BF16)
        v[:, 0:INNER] = fields[:, 1152:WIDTH].astype(BF16)

    def window(h):
        first = (HEAD_DIM * h) // 128
        lane = lax.broadcasted_iota(jnp.int32, (1, 256), 1) + first * 128 - HEAD_DIM * h
        keep = jnp.where((lane >= 0) & (lane < HEAD_DIM), 1.0, 0.0).astype(BF16)
        return pl.ds(pl.multiple_of(first * 128, 128), 256), keep

    def forward(q, k, v, probs, mixed, same_patch):
        mixed[...] = jnp.zeros_like(mixed)

        def head(h, carry):
            cols, keep = window(h)
            scores = dot(q[:, cols], k[:, cols] * keep, ((1,), (1,))) * SCALING
            if same_patch:
                a = lax.broadcasted_iota(jnp.int32, scores.shape, 0)
                b = lax.broadcasted_iota(jnp.int32, scores.shape, 1)
                scores = jnp.where(((a ^ b) & (GROUP - 1)) == 0, scores, -1e30)
            weights = jnp.exp(scores - jnp.max(scores, axis=1, keepdims=True))
            p = weights / jnp.sum(weights, axis=1, keepdims=True)
            probs[h] = p
            mixed[:, cols] += dot(p.astype(BF16), v[:, cols] * keep)
            return carry

        lax.fori_loop(0, HEADS, head, 0)

    def backward(q, k, v, dm, probs, dq, dk, dv):
        for out in (dq, dk, dv):
            out[...] = jnp.zeros_like(out)

        def head(h, carry):
            cols, keep = window(h)
            p = probs[h]
            dm_h = dm[:, cols] * keep
            dv[:, cols] += dot(p.astype(BF16), dm_h, ((0,), (0,)))
            dp = dot(dm_h, v[:, cols], ((1,), (1,)))
            dsc = (p * (dp - jnp.sum(dp * p, axis=1, keepdims=True))).astype(BF16)
            dq[:, cols] += dot(dsc, k[:, cols] * keep)
            dk[:, cols] += dot(dsc, q[:, cols] * keep, ((0,), (0,)))
            return carry

        lax.fori_loop(0, HEADS, head, 0)

    def joined(dq, dk, dv, store):
        a = dq[...] * SCALING
        b = pltpu.roll(dk[...] * SCALING, 64, 1)
        store(0, 512, a[:, 0:512])
        store(512, 640, a[:, 512:PAD] + b[:, 0:128])
        store(640, 1152, b[:, 128:PAD])
        store(1152, WIDTH, dv[:, 0:INNER])

    local[0].wait()
    split(qkvs[...].astype(F32), qs, ks, vs)
    forward(qs, ks, vs, probs_s, acc0, False)

    def rows_x(b):
        return [
            remote(
                wbuf.at[b, x], wbuf.at[b, x], wx_s.at[b, step], wx_r.at[b, step], at_x(step)
            )
            for step in (1, 2, 3)
        ]

    wx = [rows_x(b) for b in (0, 1)]
    for b in (1, 0):
        local[3 + b].wait()
        for copy in wz[b]:
            copy.wait_recv()
        for copy in wx[b]:
            copy.start()

    def mixed_start(b, mixed):
        m2[b, 0:PATCHES, :] = dot(mixed, sel[0], ((1,), (1,))).astype(BF16)
        mx[b] = dot(mixed, sel[1], ((1,), (1,))).astype(BF16)
        copy = remote(
            mx.at[b], m2.at[b, pl.ds(PATCHES, PATCHES)], p_s.at[b], p_r.at[b], partner
        )
        copy.start()
        return copy

    def reduce_y_start(b):
        gstage[...] = dot(m2[b], og2[...], ((0,), (0,))) * FACTOR

        def put(i, carry):
            rows = pl.ds(pl.multiple_of(i * BLOCK, BLOCK), BLOCK)
            gbuf[b, lax.rem(i, 4), i // 4] = gstage[rows, :][0:ROWS].astype(BF16)
            return carry

        lax.fori_loop(0, 16, put, 0)
        copies = [
            remote(
                gbuf.at[b, lax.rem(y + step, 4)], yrecv.at[b, step],
                y_s.at[b, step], y_r.at[b, step], at_y(step),
            )
            for step in (1, 2, 3)
        ]
        for copy in copies:
            copy.start()
        return copies

    def reduce_x_start(b, copies):
        for copy in copies:
            copy.wait()
        for i in range(4):
            total = gbuf[b, y, i].astype(F32)
            for step in (1, 2, 3):
                total += yrecv[b, step, i].astype(F32)
            xbuf[b, i] = total.astype(BF16)
        copies = [
            remote(
                xbuf.at[b, lax.rem(x + step, 4)], xrecv.at[b, step],
                x_s.at[b, step], x_r.at[b, step], at_x(step),
            )
            for step in (1, 2, 3)
        ]
        for copy in copies:
            copy.start()
        return copies

    def reduce_z_start(b, copies):
        for copy in copies:
            copy.wait()
        total = xbuf[b, x].astype(F32)
        for step in (1, 2, 3):
            total += xrecv[b, step].astype(F32)
        zbuf[b] = total.astype(BF16)

        @pl.when(zl != y)
        def _():
            gather_z(b, 0).start()

    def gather_z(b, step):
        slot = lax.rem(zl - y + 4, 4) if step == 0 else step
        return remote(
            zbuf.at[b], zrecv.at[b, slot], z_s.at[b], z_r.at[b, slot],
            at(rep, y * 8 + lax.rem(me, 8)),
        )

    def spread_zh(b):
        return [
            remote(
                z2buf.at[b], z2recv.at[b, step], zz_s.at[b, step], zz_r.at[b, step], at_zh(step)
            )
            for step in (1, 2, 3)
        ]

    def reduce_zh_start(b):
        @pl.when(zl != y)
        def _():
            gather_z(b, 0).wait_send()

        @pl.when(zl == y)
        def _():
            total = zbuf[b].astype(F32)
            for step in (1, 2, 3):
                gather_z(b, step).wait_recv()
                total += zrecv[b, step].astype(F32)
            z2buf[b] = total.astype(BF16)
            for copy in spread_zh(b):
                copy.start()

    def spread_y(b):
        return [
            remote(res.at[b], res.at[b], f_s.at[b, step], f_r.at[b], at_y(step))
            for step in (1, 2, 3)
        ]

    def spread_start(b):
        @pl.when(zl == y)
        def _():
            total = z2buf[b].astype(F32)
            for step, copy in zip((1, 2, 3), spread_zh(b), strict=True):
                copy.wait()
                total += z2recv[b, step].astype(F32)
            res[b] = total.astype(BF16)
            for copy in spread_y(b):
                copy.start()

    def spread_end(b):
        @pl.when(zl == y)
        def _():
            for copy in spread_y(b):
                copy.wait_send()

        @pl.when(zl != y)
        def _():
            spread_y(b)[0].wait_recv()

    mixed_s = mixed_start(0, acc0[...].astype(BF16))

    def grad_mixed(b):
        for copy in wx[b]:
            copy.wait_recv()

        def put(i, carry):
            rows = pl.ds(pl.multiple_of(i * BLOCK, BLOCK), BLOCK)
            block = wbuf[b, i // 4, lax.rem(i, 4)].astype(F32)
            wf[rows, :] = jnp.concatenate([block, jnp.zeros((BLOCK - ROWS, D), F32)], axis=0)
            return carry

        lax.fori_loop(0, 16, put, 0)
        wmat[...] = wf[...].astype(BF16)
        dah[b] = dot(og2[...], wmat[...], ((1,), (1,))).astype(BF16)
        copy = remote(
            dah.at[b, pl.ds(PATCHES, PATCHES)], dax.at[b], p_s.at[2 + b], p_r.at[2 + b], partner
        )
        copy.start()
        mine = dot(dah[b, 0:PATCHES, :], sel[0])
        copy.wait()
        return mine + dot(dax[b], sel[1])

    local[1].wait()
    og_copy.wait()
    dmt = grad_mixed(1)
    das[...] = dmt[:, 0:INNER].reshape(FRAMES, GROUP, INNER).astype(BF16)
    grads_out[0]()
    own = [
        pltpu.make_async_copy(das.at[me], dar.at[me], lsem.at[5]),
        pltpu.make_async_copy(mts.at[me], mtr.at[me], lsem.at[6]),
        pltpu.make_async_copy(gts.at[me], gt_ref.at[me], lsem.at[7]),
        pltpu.make_async_copy(res, gw_ref, lsem.at[8]),
        pltpu.make_async_copy(qkvs, gs_ref, lsem.at[9]),
    ]
    own[0].start()

    mixed_s.wait()
    share_s = reduce_y_start(0)

    local[2].wait()
    fields_out[1]()
    split(qtr[...].astype(F32).reshape(PATCHES, WIDTH), qt, kt, vt)
    forward(qt, kt, vt, probs_t, acc0, True)
    mts[...] = acc0[:, 0:INNER].reshape(FRAMES, GROUP, INNER).astype(BF16)
    mixed_back[0]()
    own[1].start()

    share_s = reduce_x_start(0, share_s)

    own[0].wait()
    grads_out[1]()
    dt[:, 512:PAD] = jnp.zeros((PATCHES, PAD - 512), BF16)
    dt[:, 0:INNER] = dar[...].astype(F32).reshape(PATCHES, INNER).astype(BF16)
    backward(qt, kt, vt, dt, probs_t, acc0, acc1, acc2)

    def put_temporal(low, high, value):
        gts[:, :, low:high] = value.reshape(FRAMES, GROUP, high - low).astype(BF16)

    joined(acc0, acc1, acc2, put_temporal)
    fields_back[0]()
    own[2].start()

    reduce_z_start(0, share_s)

    own[1].wait()
    mixed_back[1]()
    mixed_t = mixed_start(1, jnp.concatenate(
        [mtr[...].astype(F32).reshape(PATCHES, INNER), jnp.zeros((PATCHES, PAD - INNER), F32)], axis=1
    ).astype(BF16))
    mixed_t.wait()
    share_t = reduce_y_start(1)
    reduce_zh_start(0)

    dms = grad_mixed(0)
    ds[...] = dms.astype(BF16)
    spread_start(0)
    share_t = reduce_x_start(1, share_t)
    backward(qs, ks, vs, ds, probs_s, acc0, acc1, acc2)

    def put_spatial(low, high, value):
        qkvs[:, low:high] = value.astype(BF16)

    joined(acc0, acc1, acc2, put_spatial)
    own[4].start()

    reduce_z_start(1, share_t)
    reduce_zh_start(1)
    spread_start(1)
    spread_end(0)
    spread_end(1)
    own[3].start()

    for copy in [c for b in (0, 1) for c in wz[b] + wx[b]]:
        copy.wait_send()
    fields_out[2]()
    grads_out[2]()
    mixed_back[2]()
    fields_back[1]()
    fields_back[2]()
    for copy in own[2:]:
        copy.wait()


def per_device(qkv_spatial, qkv_temporal, out_grad, out_proj):
    def vmem(*shape, dtype=BF16):
        return pltpu.VMEM(shape, dtype)

    dma = pltpu.SemaphoreType.DMA
    scratch = [
        vmem(PATCHES, WIDTH),
        vmem(2 * PATCHES, D),
        vmem(FRAMES, GROUP, WIDTH),
        vmem(FRAMES, GROUP, INNER),
        vmem(FRAMES, GROUP, INNER),
        vmem(FRAMES, GROUP, INNER),
        vmem(FRAMES, GROUP, INNER),
        vmem(FRAMES, GROUP, WIDTH),
        vmem(2, 4, 4, ROWS, D),
        vmem(HALF, D, dtype=F32),
        vmem(HALF, D),
        vmem(2, HALF, PAD),
        vmem(2, HALF, PAD, dtype=F32),
        vmem(2, 2 * PATCHES, HALF),
        vmem(2, PATCHES, HALF),
        vmem(2, 2 * PATCHES, HALF),
        vmem(2, PATCHES, HALF),
        vmem(2, 4, 4, ROWS, D),
        vmem(2, 4, 4, ROWS, D),
        vmem(2, 4, ROWS, D),
        vmem(2, 4, ROWS, D),
        vmem(2, ROWS, D),
        vmem(2, 4, ROWS, D),
        vmem(2, ROWS, D),
        vmem(2, 4, ROWS, D),
        vmem(2, ROWS, D),
        *[vmem(PATCHES, PAD) for _ in range(8)],
        vmem(HEADS, PATCHES, PATCHES, dtype=F32),
        vmem(HEADS, PATCHES, PATCHES, dtype=F32),
        *[vmem(PATCHES, PAD, dtype=F32) for _ in range(3)],
        vmem(HALF, D, dtype=F32),
        dma((10,)),
        dma((2, 3)), dma((2, 3)),
        dma((2, 4)), dma((2, 4)),
        dma((1,)), dma((1,)),
        *[dma((SEQ,)) for _ in range(8)],
        dma((4,)), dma((4,)),
        dma((2, 4)), dma((2, 4)),
        dma((2, 4)), dma((2, 4)),
        dma((2,)), dma((2, 4)),
        dma((2, 4)), dma((2, 4)),
        dma((2, 4)), dma((2,)),
    ]
    hbm = pl.BlockSpec(memory_space=pl.ANY)
    spatial, temporal, rows = pl.pallas_call(
        kernel,
        name="attention_backward",
        out_shape=[
            jax.ShapeDtypeStruct((PATCHES, WIDTH), BF16),
            jax.ShapeDtypeStruct((FRAMES, GROUP, WIDTH), BF16),
            jax.ShapeDtypeStruct((2, ROWS, D), BF16),
        ],
        in_specs=[hbm] * 4,
        out_specs=[hbm] * 3,
        scratch_shapes=scratch,
        compiler_params=pltpu.CompilerParams(
            collective_id=0, has_side_effects=True, vmem_limit_bytes=56 * 2**20
        ),
    )(
        qkv_spatial,
        qkv_temporal.reshape(FRAMES, GROUP, WIDTH),
        out_grad,
        jnp.transpose(out_proj, (1, 0, 2)),
    )
    return spatial, temporal.reshape(PATCHES, WIDTH), jnp.transpose(rows, (1, 0, 2))


def solution(mesh):
    placed = (
        P(("rep", "seq"), None),
        P(("rep", "seq"), None),
        P(("rep", "seq"), None),
        P("seq", None, None),
    )
    return jax.shard_map(
        per_device,
        mesh=mesh,
        in_specs=placed,
        out_specs=(P(("rep", "seq"), None), P(("rep", "seq"), None), P("seq", None, None)),
        check_vma=False,
    )
```

```python
import functools

import jax
import jax.numpy as jnp
from jax import lax
from jax.experimental import pallas as pl
from jax.experimental.pallas import tpu as pltpu
from jax.sharding import PartitionSpec as P

HEADS, HEAD_DIM, PATCHES, FRAMES = 8, 72, 256, 32
INNER, WIDTH, D = 576, 1728, 1152
PART = 4
PAD = 384
FIELDS = 896
GROUP = 8
ROWS = 18
BLOCK = 24
PAIR = 40
QUAD = 4 * ROWS
HALF = 4 * QUAD
SEQ, TOKENS = 32, 131072
SCALING = HEAD_DIM**-0.5
FACTOR = float(TOKENS) ** -0.5
F32, BF16 = jnp.float32, jnp.bfloat16


def dot(left, right, dims=((1,), (0,))):
    return lax.dot_general(left, right, (dims, ((), ())), preferred_element_type=F32)


def kernel(
    qkvs_ref, qkvt_ref, og_ref, w_ref,
    gs_ref, gt_ref, gw_ref,
    qkvs, gsb, og2, qtin, qts, qtr, ogr, ogt, gts, gtr, gto, wraw, wz, wx, wmat, selw, selg, m2,
    gbuf, yrecv, ysum, xbuf, xrecv, zbuf, zrecv, z2buf, z2recv, res,
    qt, kt, vt, dt, probs_s, probs_t, acc0, acc1, acc2, mixs, dms, turn,
    lsem, wz_s, wz_r, wx_s, wx_r, ww_s, ww_r, og_s, og_r, a_s, a_r, b_s, b_r, d_s, d_r,
    p_s, p_r, y_s, y_r, x_s, x_r, z_s, z_r, zz_s, zz_r, f_s, f_r,
):
    rep, me = lax.axis_index("rep"), lax.axis_index("seq")
    zh, y = rep // 4, lax.rem(rep, 4)
    zl, x, core = me // 8, lax.rem(me // 2, 4), lax.rem(me, 2)
    z = 4 * zh + zl

    def at(rep_to, seq_to):
        return {"device_id": (rep_to, seq_to), "device_id_type": pl.DeviceIdType.MESH}

    def at_z(step):
        to = lax.rem(z + step + 16, 16)
        return at((to // 4) * 4 + y, lax.rem(to, 4) * 8 + lax.rem(me, 8))

    def at_y(step):
        return at(zh * 4 + lax.rem(y + step, 4), me)

    def at_zh(step):
        return at(lax.rem(zh + step, 4) * 4 + y, me)

    def at_x(step):
        return at(rep, zl * 8 + lax.rem(x + step, 4) * 2 + core)

    partner = at(rep, me + 1 - 2 * core)

    def remote(src, dst, send, recv, target):
        return pltpu.make_async_remote_copy(
            src_ref=src, dst_ref=dst, send_sem=send, recv_sem=recv, **target
        )

    barrier = pltpu.get_barrier_semaphore()

    def greet(k, carry):
        pl.semaphore_signal(barrier, inc=1, **at(rep, lax.rem(me + k, SEQ)))
        return carry

    lax.fori_loop(1, SEQ, greet, 0)
    for step in (-1, -2, 1):
        pl.semaphore_signal(barrier, inc=1, **at_z(step))
    for step in (1, 2, 3):
        pl.semaphore_signal(barrier, inc=1, **at_y(step))
        pl.semaphore_signal(barrier, inc=1, **at_zh(step))

    local = [
        pltpu.make_async_copy(w_ref, wraw, lsem.at[0]),
        pltpu.make_async_copy(qkvs_ref, qkvs, lsem.at[1]),
        pltpu.make_async_copy(og_ref, og2.at[0], lsem.at[2]),
        pltpu.make_async_copy(qkvt_ref, qtin, lsem.at[3]),
        pltpu.make_async_copy(og_ref.at[me], ogr.at[0, me], lsem.at[5]),
    ]
    for copy in local:
        copy.start()
    local[0].wait()
    own_rows = wraw[...].astype(F32)
    for b in (0, 1):
        wz[b, zl] = jnp.concatenate(
            [own_rows[:, b, :], jnp.zeros((BLOCK - ROWS, D), F32)], axis=0
        ).astype(BF16)

    def units(half):
        return [
            (HEAD_DIM * (PART * w + i), HEADS * w + 2 * i + half) for w in range(3) for i in range(PART)
        ]

    local[3].wait()
    turn[3 * PART * HEAD_DIM :, :] = jnp.zeros((FIELDS - 3 * PART * HEAD_DIM, PATCHES), F32)
    own_fields = []

    def turn_fields(half):
        for row, field in units(half):
            turn[row : row + HEAD_DIM, :] = qtin[field].astype(F32)
        for first in range(0, FIELDS, 128):
            part = turn[first : first + 128, :].T.reshape(FRAMES, GROUP, 128)
            qts[half, :, :, first : first + 128] = part.astype(BF16)
        copy = pltpu.make_async_copy(qts.at[half, me], qtr.at[half, me], lsem.at[9 + half])
        copy.start()
        own_fields.append(copy)

    turn_fields(0)

    pl.semaphore_wait(barrier, 31 + 9)

    def rows_z(b):
        return [
            remote(wz.at[b, zl], wz.at[b, zl], wz_s.at[b, i], wz_r.at[b, i], at_z(step))
            for i, step in enumerate((1, 2, -1))
        ]

    along_z = [rows_z(b) for b in (0, 1)]
    for copy in along_z[1] + along_z[0]:
        copy.start()

    def exchange(src, dst, send, recv):
        def copy(k):
            to = lax.rem(me + k, SEQ)
            return remote(src.at[to], dst.at[me], send.at[k], recv.at[k], at(rep, to))

        def start(k, carry):
            copy(k).start()
            return carry

        def landed(k, carry):
            copy(k).wait_recv()
            return carry

        def sent(k, carry):
            copy(k).wait_send()
            return carry

        return (
            lambda: lax.fori_loop(1, SEQ, start, 0),
            lambda: lax.fori_loop(1, SEQ, landed, 0),
            lambda: lax.fori_loop(1, SEQ, sent, 0),
        )

    fields_out = [
        exchange(qts.at[half], qtr.at[half], a_s.at[half], a_r.at[half]) for half in (0, 1)
    ]
    cotangent_out = exchange(og_ref, ogr.at[0], b_s, b_r)
    fields_back = [
        exchange(gts.at[half], gtr.at[half], d_s.at[half], d_r.at[half]) for half in (0, 1)
    ]
    fields_out[0][0]()
    cotangent_out[0]()
    turn_fields(1)
    fields_out[1][0]()
    og_copy = remote(og2.at[0], og2.at[1], og_s.at[0], og_r.at[0], partner)
    local[2].wait()
    og_copy.start()

    r = lax.broadcasted_iota(jnp.int32, (HALF, 1), 0)
    block = (r * 3641) >> 16
    high, low, j = block >> 2, block & 3, r - ROWS * block
    n = lax.broadcasted_iota(jnp.int32, (HALF, PAD), 1)
    for which in (0, 1):
        parity = core if which == 0 else 1 - core
        own = ROWS * (8 * low + 2 * high + parity) + j
        head = (own * 911) >> 16
        column = HEAD_DIM * (head >> 1) + own - HEAD_DIM * head
        for half in (0, 1):
            hit = (n == column) & ((head & 1) == half)
            selw[half, HALF * which : HALF * (which + 1), :] = jnp.where(hit, 1.0, 0.0).astype(BF16)
    r = lax.broadcasted_iota(jnp.int32, (4 * PAIR, 1), 0)
    n = lax.broadcasted_iota(jnp.int32, (4 * PAIR, PAD), 1)
    high = (r * 1639) >> 16
    low = jnp.where(r - PAIR * high >= ROWS, 1, 0)
    j = r - PAIR * high - ROWS * low
    for which in (0, 1):
        parity = core if which == 0 else 1 - core
        hit = (n == HEAD_DIM * high + ROWS * (2 * low + parity) + j) & (j < ROWS)
        selg[which] = jnp.where(hit, 1.0, 0.0).astype(BF16)
    mixs[...] = jnp.zeros_like(mixs)

    def split(half):
        fields = qtr[half].astype(F32).reshape(PATCHES, FIELDS)
        qt[half] = fields[:, 0:PAD].astype(BF16)
        kt[half] = pltpu.roll(fields[:, 256:640], PAD - 32, 1).astype(BF16)
        vt[half] = pltpu.roll(fields[:, 512:FIELDS], PAD - 64, 1).astype(BF16)

    def window(h):
        first = (HEAD_DIM * h) // 128
        lane = lax.broadcasted_iota(jnp.int32, (1, 256), 1) + first * 128 - HEAD_DIM * h
        keep = jnp.where((lane >= 0) & (lane < HEAD_DIM), 1.0, 0.0).astype(BF16)
        return pl.ds(pl.multiple_of(first * 128, 128), 256), keep

    def forward(half):
        q, k, v = qt.at[half], kt.at[half], vt.at[half]
        acc0[...] = jnp.zeros_like(acc0)

        def head(h, carry):
            cols, keep = window(h)
            scores = dot(q[:, cols], k[:, cols] * keep, ((1,), (1,))) * SCALING
            a = lax.broadcasted_iota(jnp.int32, scores.shape, 0)
            b = lax.broadcasted_iota(jnp.int32, scores.shape, 1)
            scores = jnp.where(((a ^ b) & (GROUP - 1)) == 0, scores, -1e30)
            weights = jnp.exp(scores - jnp.max(scores, axis=1, keepdims=True))
            p = weights / jnp.sum(weights, axis=1, keepdims=True)
            probs_t[PART * half + h] = p
            acc0[:, cols] += dot(p.astype(BF16), v[:, cols] * keep)
            return carry

        lax.fori_loop(0, PART, head, 0, unroll=2)

    def backward(half):
        q, k, v, dm = qt.at[half], kt.at[half], vt.at[half], dt.at[half]
        for out in (acc0, acc1, acc2):
            out[...] = jnp.zeros_like(out)

        def head(h, carry):
            cols, keep = window(h)
            p = probs_t[PART * half + h]
            dm_h = dm[:, cols] * keep
            acc2[:, cols] += dot(p.astype(BF16), dm_h, ((0,), (0,)))
            dp = dot(dm_h, v[:, cols], ((1,), (1,)))
            dsc = (p * (dp - jnp.sum(dp * p, axis=1, keepdims=True))).astype(BF16)
            acc0[:, cols] += dot(dsc, k[:, cols] * keep)
            acc1[:, cols] += dot(dsc, q[:, cols] * keep, ((0,), (0,)))
            return carry

        lax.fori_loop(0, PART, head, 0, unroll=2)
        a = acc0[...] * SCALING
        b = pltpu.roll(acc1[...] * SCALING, 32, 1)
        c = pltpu.roll(acc2[...], 64, 1)

        def put(low, value):
            high = low + value.shape[1]
            gts[half, :, :, low:high] = value.reshape(FRAMES, GROUP, high - low).astype(BF16)

        put(0, a[:, 0:256])
        put(256, a[:, 256:PAD] + b[:, 0:128])
        put(384, b[:, 128:256])
        put(512, b[:, 256:PAD] + c[:, 0:128])
        put(640, c[:, 128:PAD])
        fields_back[half][0]()
        own[half].start()

    def forward_spatial(h, carry):
        scores = dot(qkvs[h], qkvs[HEADS + h], ((0,), (0,))) * SCALING
        weights = jnp.exp(scores - jnp.max(scores, axis=1, keepdims=True))
        p = weights / jnp.sum(weights, axis=1, keepdims=True)
        probs_s[h] = p
        rows = pl.ds(pl.multiple_of((h >> 1) * HEAD_DIM, 8), HEAD_DIM)
        mixs[h & 1, rows, :] = dot(qkvs[2 * HEADS + h], p.astype(BF16), ((1,), (1,)))
        return carry

    def backward_spatial(h, carry):
        p = probs_s[h]
        rows = pl.ds(pl.multiple_of((h >> 1) * HEAD_DIM, 8), HEAD_DIM)
        dm_h = dms[h & 1, rows, :].astype(BF16)
        dv = dot(dm_h, p.astype(BF16))
        dp = dot(dm_h, qkvs[2 * HEADS + h], ((0,), (0,)))
        dsc = (p * (dp - jnp.sum(dp * p, axis=1, keepdims=True))).astype(BF16)
        dq = dot(qkvs[HEADS + h], dsc, ((1,), (1,))) * SCALING
        dk = dot(qkvs[h], dsc) * SCALING
        gsb[h] = dq.astype(BF16)
        gsb[HEADS + h] = dk.astype(BF16)
        gsb[2 * HEADS + h] = dv.astype(BF16)
        return carry

    def rows_x(b):
        return [
            remote(
                wx.at[0, b, x], wx.at[0, b, x], wx_s.at[b, step], wx_r.at[b, step], at_x(step)
            )
            for step in (1, 2, 3)
        ]

    along_x = [rows_x(b) for b in (0, 1)]

    def rows_x_start(b):
        for copy in along_z[b]:
            copy.wait_recv()
        parts = [wz[b, i].astype(F32)[0:ROWS] for i in range(4)]
        wx[0, b, x] = jnp.concatenate(parts, axis=0).astype(BF16)
        for copy in along_x[b]:
            copy.start()

    to_partner = [
        remote(wx.at[0, b], wx.at[1, b], ww_s.at[b], ww_r.at[b], partner) for b in (0, 1)
    ]

    def rows_swap(b):
        for copy in along_x[b]:
            copy.wait_recv()
        to_partner[b].start()

    def rows_all(b):
        to_partner[b].wait_recv()
        for which in (0, 1):
            half = wx[which, b].astype(F32).reshape(HALF, D).astype(BF16)
            wmat[HALF * which : HALF * (which + 1), :] = half

    local[1].wait()
    lax.fori_loop(0, HEADS, forward_spatial, 0, unroll=2)

    def mixed_start(u, mixed, dims):
        m2[u, 0] = dot(selg[0], mixed, dims).astype(BF16)
        m2[u, 1] = dot(selg[1], mixed, dims).astype(BF16)
        copy = remote(m2.at[u, 1], m2.at[u, 2], p_s.at[u], p_r.at[u], partner)
        copy.start()
        return copy

    def flat(rows):
        return rows.astype(F32).reshape(PATCHES, D).astype(BF16)

    def along(u):
        return [
            remote(
                gbuf.at[u, (y + step) & 3], yrecv.at[u, step],
                y_s.at[u, step], y_r.at[u, step], at_y(step),
            )
            for step in (1, 2, 3)
        ]

    def reduce_y_start(u, cotangents):
        share = dot(m2[u, 0], cotangents[0]) + dot(m2[u, 2], cotangents[1])
        gbuf[u] = (share * FACTOR).reshape(4, PAIR, D).astype(BF16)
        for copy in along(u):
            copy.start()

    def send_x(u, i):
        to = 2 * (u & 1) + i
        return to, remote(
            xbuf.at[u, i], xrecv.at[u, (x - to) & 3],
            x_s.at[u, i], x_r.at[u, (x - to) & 3], at(rep, zl * 8 + to * 2 + core),
        )

    def reduce_x_start(u):
        for copy in along(u):
            copy.wait()
        total = gbuf[u, y].astype(F32)
        for step in (1, 2, 3):
            total += yrecv[u, step].astype(F32)
        ysum[...] = total
        for i in (0, 1):
            rows = ysum[ROWS * i : ROWS * (i + 1), :]
            xbuf[u, i] = jnp.concatenate(
                [rows, jnp.zeros((BLOCK - ROWS, D), F32)], axis=0
            ).astype(BF16)
            to, copy = send_x(u, i)
            pl.when(x != to)(copy.start)

    def reduce_x_end(u):
        for i in (0, 1):
            to, copy = send_x(u, i)
            pl.when(x != to)(copy.wait_send)

    def here(u):
        return (x >> 1) == (u & 1)

    def reduce_z_start(u):
        b = u >> 1

        @pl.when(here(u))
        def _():
            total = xbuf[u, x & 1].astype(F32)
            for step in (1, 2, 3):
                arrived = xrecv.at[u, step]
                remote(arrived, arrived, x_s.at[u, 0], x_r.at[u, step], partner).wait_recv()
                total += xrecv[u, step].astype(F32)
            zbuf[b] = total.astype(BF16)
            pl.when(zl != y)(gather_z(b, 0).start)

    def gather_z(b, step):
        slot = lax.rem(zl - y + 4, 4) if step == 0 else step
        return remote(
            zbuf.at[b], zrecv.at[b, slot], z_s.at[b], z_r.at[b, slot],
            at(rep, y * 8 + lax.rem(me, 8)),
        )

    def spread_zh(b):
        return [
            remote(
                z2buf.at[b], z2recv.at[b, step], zz_s.at[b, step], zz_r.at[b, step], at_zh(step)
            )
            for step in (1, 2, 3)
        ]

    def reduce_zh_start(u):
        b = u >> 1

        @pl.when(here(u))
        def _stage():
            @pl.when(zl != y)
            def _():
                gather_z(b, 0).wait_send()

            @pl.when(zl == y)
            def _():
                total = zbuf[b].astype(F32)
                for step in (1, 2, 3):
                    gather_z(b, step).wait_recv()
                    total += zrecv[b, step].astype(F32)
                z2buf[b] = total.astype(BF16)
                for copy in spread_zh(b):
                    copy.start()

    def spread_y(b):
        return [
            remote(res.at[b], res.at[b], f_s.at[b, step], f_r.at[b], at_y(step))
            for step in (1, 2, 3)
        ]

    def spread_start(u):
        b = u >> 1

        @pl.when(here(u))
        def _stage():
            @pl.when(zl == y)
            def _():
                total = z2buf[b].astype(F32)
                for step, copy in zip((1, 2, 3), spread_zh(b), strict=True):
                    copy.wait()
                    total += z2recv[b, step].astype(F32)
                res[b] = total.astype(BF16)
                for copy in spread_y(b):
                    copy.start()

    def spread_end(u):
        b = u >> 1

        @pl.when(here(u))
        def _stage():
            @pl.when(zl == y)
            def _():
                for copy in spread_y(b):
                    copy.wait_send()

            @pl.when(zl != y)
            def _():
                spread_y(b)[0].wait_recv()

    swap_s = [mixed_start(half, mixs[half].astype(BF16), ((1,), (0,))) for half in (0, 1)]
    rows_x_start(1)
    own = [
        pltpu.make_async_copy(gts.at[0, me], gtr.at[0, me], lsem.at[4]),
        pltpu.make_async_copy(gts.at[1, me], gtr.at[1, me], lsem.at[6]),
        pltpu.make_async_copy(gsb, gs_ref, lsem.at[7]),
        pltpu.make_async_copy(gto, gt_ref, lsem.at[8]),
        pltpu.make_async_copy(res, gw_ref, lsem.at[11]),
    ]
    og_copy.wait()
    ogt[0] = flat(og2[0])
    ogt[1] = flat(og2[1])
    for half in (0, 1):
        swap_s[half].wait()
        reduce_y_start(half, (ogt[0], ogt[1]))
    rows_swap(1)

    def forward_half(half):
        own_fields[half].wait()
        fields_out[half][1]()
        split(half)
        forward(half)
        return mixed_start(2 + half, acc0[...].astype(BF16), ((1,), (1,)))

    for half in (0, 1):
        reduce_x_start(half)
    swap_t = forward_half(0)
    for half in (0, 1):
        reduce_z_start(half)
    rows_all(1)
    rows_x_start(0)

    local[4].wait()
    cotangent_out[1]()
    ogr_copy = remote(ogr.at[0], ogr.at[1], og_s.at[1], og_r.at[1], partner)
    ogr_copy.start()
    ogt[0] = flat(ogr[0])
    dah = dot(ogt[0], wmat[...], ((1,), (1,))).astype(BF16)
    for half in (0, 1):
        dt[half] = dot(dah, selw[half]).astype(BF16)
    swap_t.wait()
    ogr_copy.wait()
    ogt[1] = flat(ogr[1])
    reduce_y_start(2, (ogt[0], ogt[1]))
    for half in (0, 1):
        reduce_zh_start(half)
    rows_swap(0)
    backward(0)
    reduce_x_start(2)

    swap_t = forward_half(1)
    reduce_z_start(2)
    swap_t.wait()
    reduce_y_start(3, (ogt[0], ogt[1]))
    backward(1)
    reduce_x_start(3)
    reduce_z_start(3)
    for half in (0, 1):
        spread_start(half)
    reduce_zh_start(2)

    def turn_back(half):
        own[half].wait()
        fields_back[half][1]()
        for first in range(0, FIELDS, 128):
            part = gtr[half, :, :, first : first + 128].astype(F32)
            turn[first : first + 128, :] = part.reshape(PATCHES, 128).T
        for row, field in units(half):
            gto[field] = turn[row : row + HEAD_DIM, :].astype(BF16)
    turn_back(0)
    reduce_zh_start(3)
    spread_start(2)

    rows_all(0)
    dah = dot(wmat[...], flat(og2[0]), ((1,), (1,))).astype(BF16)
    for half in (0, 1):
        dms[half] = dot(selw[half], dah, ((0,), (0,)))
    lax.fori_loop(0, HEADS, backward_spatial, 0, unroll=2)
    own[2].start()

    spread_start(3)
    turn_back(1)
    own[3].start()
    for u in range(4):
        spread_end(u)
    own[4].start()

    for copy in [c for b in (0, 1) for c in along_z[b] + along_x[b] + [to_partner[b]]]:
        copy.wait_send()
    for u in range(4):
        reduce_x_end(u)
    cotangent_out[2]()
    for half in (0, 1):
        fields_out[half][2]()
        fields_back[half][2]()
    for copy in own[2:]:
        copy.wait()


def finish(gs_ref, gt_ref, rows_ref, gs_out, gt_out, rows_out, fields, rows, sems):
    load = [pltpu.make_async_copy(rows_ref, rows, sems.at[0])]
    store = []
    for i, (src, dst) in enumerate(((gs_ref, gs_out), (gt_ref, gt_out))):
        for w in range(3):
            part, k = pl.ds(HEADS * w, HEADS), 3 * i + w
            load.append(pltpu.make_async_copy(src.at[part], fields.at[k], sems.at[1 + k]))
            store.append(pltpu.make_async_copy(fields.at[k], dst.at[part], sems.at[7 + k]))
    for copy in load:
        copy.start()
    load[0].wait()
    both = [rows[b].astype(F32)[0:ROWS] for b in (0, 1)]
    rows_out[...] = jnp.stack(both, axis=1).astype(BF16)
    for arrived, copy in zip(load[1:], store, strict=True):
        arrived.wait()
        copy.start()
    for copy in store:
        copy.wait()


def per_device(qkv_spatial, qkv_temporal, out_grad, out_proj):
    def vmem(*shape, dtype=BF16):
        return pltpu.VMEM(shape, dtype)

    dma = pltpu.SemaphoreType.DMA
    scratch = [
        vmem(3 * HEADS, HEAD_DIM, PATCHES),
        vmem(3 * HEADS, HEAD_DIM, PATCHES),
        vmem(2, FRAMES, GROUP, D),
        vmem(3 * HEADS, HEAD_DIM, PATCHES),
        vmem(2, FRAMES, GROUP, FIELDS),
        vmem(2, FRAMES, GROUP, FIELDS),
        vmem(2, FRAMES, GROUP, D),
        vmem(2, PATCHES, D),
        vmem(2, FRAMES, GROUP, FIELDS),
        vmem(2, FRAMES, GROUP, FIELDS),
        vmem(3 * HEADS, HEAD_DIM, PATCHES),
        vmem(ROWS, 2, D),
        vmem(2, 4, BLOCK, D),
        vmem(2, 2, 4, QUAD, D),
        vmem(INNER, D),
        vmem(2, INNER, PAD),
        vmem(2, 4 * PAIR, PAD),
        vmem(4, 3, 4 * PAIR, PATCHES),
        vmem(4, 4, PAIR, D),
        vmem(4, 4, PAIR, D),
        vmem(PAIR, D, dtype=F32),
        vmem(4, 2, BLOCK, D),
        vmem(4, 4, BLOCK, D),
        vmem(2, BLOCK, D),
        vmem(2, 4, BLOCK, D),
        vmem(2, BLOCK, D),
        vmem(2, 4, BLOCK, D),
        vmem(2, BLOCK, D),
        *[vmem(2, PATCHES, PAD) for _ in range(4)],
        vmem(HEADS, PATCHES, PATCHES, dtype=F32),
        vmem(HEADS, PATCHES, PATCHES, dtype=F32),
        *[vmem(PATCHES, PAD, dtype=F32) for _ in range(3)],
        *[vmem(2, PAD, PATCHES, dtype=F32) for _ in range(2)],
        vmem(FIELDS, PATCHES, dtype=F32),
        dma((12,)),
        dma((2, 3)), dma((2, 3)),
        dma((2, 4)), dma((2, 4)),
        dma((2,)), dma((2,)),
        dma((2,)), dma((2,)),
        dma((2, SEQ)), dma((2, SEQ)),
        dma((SEQ,)), dma((SEQ,)),
        dma((2, SEQ)), dma((2, SEQ)),
        dma((4,)), dma((4,)),
        dma((4, 4)), dma((4, 4)),
        dma((4, 2)), dma((4, 4)),
        dma((2,)), dma((2, 4)),
        dma((2, 4)), dma((2, 4)),
        dma((2, 4)), dma((2,)),
    ]
    hbm = pl.BlockSpec(memory_space=pl.ANY)
    spatial, temporal, rows = pl.pallas_call(
        kernel,
        name="attention_backward",
        out_shape=[
            jax.ShapeDtypeStruct((3 * HEADS, HEAD_DIM, PATCHES), BF16),
            jax.ShapeDtypeStruct((3 * HEADS, HEAD_DIM, PATCHES), BF16),
            jax.ShapeDtypeStruct((2, BLOCK, D), BF16),
        ],
        in_specs=[hbm] * 4,
        out_specs=[hbm] * 3,
        scratch_shapes=scratch,
        compiler_params=pltpu.CompilerParams(
            collective_id=0, has_side_effects=True, vmem_limit_bytes=56 * 2**20
        ),
    )(
        qkv_spatial.T.reshape(3 * HEADS, HEAD_DIM, PATCHES),
        qkv_temporal.T.reshape(3 * HEADS, HEAD_DIM, PATCHES),
        out_grad.reshape(FRAMES, GROUP, D),
        out_proj,
    )
    spatial, temporal, rows = pl.pallas_call(
        finish,
        name="finish",
        out_shape=[
            jax.ShapeDtypeStruct((3 * HEADS, HEAD_DIM, PATCHES), BF16),
            jax.ShapeDtypeStruct((3 * HEADS, HEAD_DIM, PATCHES), BF16),
            jax.ShapeDtypeStruct((ROWS, 2, D), BF16),
        ],
        in_specs=[hbm] * 3,
        out_specs=[hbm, hbm, pl.BlockSpec(memory_space=pltpu.VMEM)],
        scratch_shapes=[vmem(6, HEADS, HEAD_DIM, PATCHES), vmem(2, BLOCK, D), dma((13,))],
        compiler_params=pltpu.CompilerParams(vmem_limit_bytes=56 * 2**20),
    )(spatial, temporal, rows)
    return spatial.reshape(WIDTH, PATCHES).T, temporal.reshape(WIDTH, PATCHES).T, rows


def solution(mesh):
    placed = (
        P(("rep", "seq"), None),
        P(("rep", "seq"), None),
        P(("rep", "seq"), None),
        P("seq", None, None),
    )
    return jax.shard_map(
        per_device,
        mesh=mesh,
        in_specs=placed,
        out_specs=(P(("rep", "seq"), None), P(("rep", "seq"), None), P("seq", None, None)),
        check_vma=False,
    )
```

```python
import functools

import jax
import jax.numpy as jnp
from jax import lax
from jax.experimental import pallas as pl
from jax.experimental.pallas import tpu as pltpu
from jax.sharding import PartitionSpec as P

HEADS, HEAD_DIM, PATCHES, FRAMES = 8, 72, 256, 32
INNER, WIDTH, D = 576, 1728, 1152
PART = 4
PAD = 384
FIELDS = 896
GROUP = 8
ROWS = 18
BLOCK = 24
PAIR = 40
QUAD = 4 * ROWS
HALF = 4 * QUAD
SEQ, TOKENS = 32, 131072
SCALING = HEAD_DIM**-0.5
FACTOR = float(TOKENS) ** -0.5
F32, BF16 = jnp.float32, jnp.bfloat16


def dot(left, right, dims=((1,), (0,))):
    return lax.dot_general(left, right, (dims, ((), ())), preferred_element_type=F32)


def kernel(
    qkvs_ref, qkvt_ref, og_ref, w_ref,
    gs_ref, gt_ref, gw_ref,
    qkvs, gsb, og2, qtin, qts, qtr, ogr, ogt, gts, gtr, gto, wraw, wown, wz, wx, wmat, selw, selg, m2,
    gbuf, yrecv, ysum, xbuf, xrecv, zbuf, zrecv, z2buf, z2recv, res,
    qt, kt, vt, dt, probs_s, probs_t, acc0, acc1, acc2, mixs, dms, turn,
    lsem, wz_s, wz_r, wy_s, wy_r, wx_s, wx_r, ww_s, ww_r, og_s, og_r, a_s, a_r, b_s, b_r, d_s, d_r,
    p_s, p_r, y_s, y_r, x_s, x_r, z_s, z_r, zz_s, zz_r, f_s, f_r,
):
    rep, me = lax.axis_index("rep"), lax.axis_index("seq")
    zh, y = rep // 4, lax.rem(rep, 4)
    zl, x, core = me // 8, lax.rem(me // 2, 4), lax.rem(me, 2)
    z = 4 * zh + zl

    def at(rep_to, seq_to):
        return {"device_id": (rep_to, seq_to), "device_id_type": pl.DeviceIdType.MESH}

    def at_z(step):
        to = lax.rem(z + step + 16, 16)
        return at((to // 4) * 4 + y, lax.rem(to, 4) * 8 + lax.rem(me, 8))

    def at_y(step):
        return at(zh * 4 + lax.rem(y + step, 4), me)

    def at_zh(step):
        return at(lax.rem(zh + step, 4) * 4 + y, me)

    def at_x(step):
        return at(rep, zl * 8 + lax.rem(x + step, 4) * 2 + core)

    partner = at(rep, me + 1 - 2 * core)

    def remote(src, dst, send, recv, target):
        return pltpu.make_async_remote_copy(
            src_ref=src, dst_ref=dst, send_sem=send, recv_sem=recv, **target
        )

    barrier = pltpu.get_barrier_semaphore()

    def greet(k, carry):
        pl.semaphore_signal(barrier, inc=1, **at(rep, lax.rem(me + k, SEQ)))
        return carry

    lax.fori_loop(1, SEQ, greet, 0)
    for step in (-1, -2, 1):
        pl.semaphore_signal(barrier, inc=1, **at_z(step))
    for step in (1, 2, 3):
        pl.semaphore_signal(barrier, inc=1, **at_y(step))
        pl.semaphore_signal(barrier, inc=1, **at_zh(step))

    local = [
        pltpu.make_async_copy(w_ref, wraw, lsem.at[0]),
        pltpu.make_async_copy(qkvs_ref, qkvs, lsem.at[1]),
        pltpu.make_async_copy(og_ref, og2.at[0], lsem.at[2]),
        pltpu.make_async_copy(qkvt_ref, qtin, lsem.at[3]),
        pltpu.make_async_copy(og_ref.at[me], ogr.at[0, me], lsem.at[5]),
    ]
    for copy in local:
        copy.start()
    local[0].wait()
    own_rows = wraw[...].astype(F32)
    rest = jnp.zeros((PAIR - 2 * ROWS, D), F32)
    own_rows = jnp.concatenate([own_rows[:, 0, :], own_rows[:, 1, :], rest], axis=0)
    wown[...] = own_rows.astype(BF16)

    @pl.when(zl == y)
    def _():
        wz[y] = wown[...]

    def units(half):
        return [
            (HEAD_DIM * (PART * w + i), HEADS * w + 2 * i + half) for w in range(3) for i in range(PART)
        ]

    local[3].wait()
    turn[3 * PART * HEAD_DIM :, :] = jnp.zeros((FIELDS - 3 * PART * HEAD_DIM, PATCHES), F32)
    own_fields = []

    def turn_fields(half):
        for row, field in units(half):
            turn[row : row + HEAD_DIM, :] = qtin[field].astype(F32)
        for first in range(0, FIELDS, 128):
            part = turn[first : first + 128, :].T.reshape(FRAMES, GROUP, 128)
            qts[half, :, :, first : first + 128] = part.astype(BF16)
        copy = pltpu.make_async_copy(qts.at[half, me], qtr.at[half, me], lsem.at[9 + half])
        copy.start()
        own_fields.append(copy)

    turn_fields(0)

    pl.semaphore_wait(barrier, 31 + 9)

    along_z = [
        remote(wown, wz.at[y], wz_s.at[i], wz_r.at[0], at_z(step))
        for i, step in enumerate((1, 2, -1))
    ]
    along_y = [
        remote(wz.at[y], wz.at[y], wy_s.at[step], wy_r.at[step], at_y(step))
        for step in (1, 2, 3)
    ]

    @pl.when(zl == y)
    def _():
        for copy in along_z + along_y:
            copy.start()

    def exchange(src, dst, send, recv):
        def copy(k):
            to = lax.rem(me + k, SEQ)
            return remote(src.at[to], dst.at[me], send.at[k], recv.at[k], at(rep, to))

        def start(k, carry):
            copy(k).start()
            return carry

        def landed(k, carry):
            copy(k).wait_recv()
            return carry

        def sent(k, carry):
            copy(k).wait_send()
            return carry

        return (
            lambda: lax.fori_loop(1, SEQ, start, 0),
            lambda: lax.fori_loop(1, SEQ, landed, 0),
            lambda: lax.fori_loop(1, SEQ, sent, 0),
        )

    fields_out = [
        exchange(qts.at[half], qtr.at[half], a_s.at[half], a_r.at[half]) for half in (0, 1)
    ]
    cotangent_out = exchange(og_ref, ogr.at[0], b_s, b_r)
    fields_back = [
        exchange(gts.at[half], gtr.at[half], d_s.at[half], d_r.at[half]) for half in (0, 1)
    ]
    fields_out[0][0]()
    cotangent_out[0]()
    turn_fields(1)
    fields_out[1][0]()

    @pl.when(zl != y)
    def _():
        along_z[0].wait_recv()
        for copy in along_y:
            copy.start()

    og_copy = remote(og2.at[0], og2.at[1], og_s.at[0], og_r.at[0], partner)
    local[2].wait()
    og_copy.start()

    r = lax.broadcasted_iota(jnp.int32, (HALF, 1), 0)
    block = (r * 3641) >> 16
    high, low, j = block >> 2, block & 3, r - ROWS * block
    n = lax.broadcasted_iota(jnp.int32, (HALF, PAD), 1)
    for which in (0, 1):
        parity = core if which == 0 else 1 - core
        own = ROWS * (8 * low + 2 * high + parity) + j
        head = (own * 911) >> 16
        column = HEAD_DIM * (head >> 1) + own - HEAD_DIM * head
        for half in (0, 1):
            hit = (n == column) & ((head & 1) == half)
            selw[half, HALF * which : HALF * (which + 1), :] = jnp.where(hit, 1.0, 0.0).astype(BF16)
    r = lax.broadcasted_iota(jnp.int32, (4 * PAIR, 1), 0)
    n = lax.broadcasted_iota(jnp.int32, (4 * PAIR, PAD), 1)
    high = (r * 1639) >> 16
    low = jnp.where(r - PAIR * high >= ROWS, 1, 0)
    j = r - PAIR * high - ROWS * low
    for which in (0, 1):
        parity = core if which == 0 else 1 - core
        hit = (n == HEAD_DIM * high + ROWS * (2 * low + parity) + j) & (j < ROWS)
        selg[which] = jnp.where(hit, 1.0, 0.0).astype(BF16)
    mixs[...] = jnp.zeros_like(mixs)

    def split(half):
        fields = qtr[half].astype(F32).reshape(PATCHES, FIELDS)
        qt[half] = fields[:, 0:PAD].astype(BF16)
        kt[half] = pltpu.roll(fields[:, 256:640], PAD - 32, 1).astype(BF16)
        vt[half] = pltpu.roll(fields[:, 512:FIELDS], PAD - 64, 1).astype(BF16)

    def window(h):
        first = (HEAD_DIM * h) // 128
        lane = lax.broadcasted_iota(jnp.int32, (1, 256), 1) + first * 128 - HEAD_DIM * h
        keep = jnp.where((lane >= 0) & (lane < HEAD_DIM), 1.0, 0.0).astype(BF16)
        return pl.ds(pl.multiple_of(first * 128, 128), 256), keep

    def forward(half):
        q, k, v = qt.at[half], kt.at[half], vt.at[half]
        acc0[...] = jnp.zeros_like(acc0)

        def head(h, carry):
            cols, keep = window(h)
            scores = dot(q[:, cols], k[:, cols] * keep, ((1,), (1,))) * SCALING
            a = lax.broadcasted_iota(jnp.int32, scores.shape, 0)
            b = lax.broadcasted_iota(jnp.int32, scores.shape, 1)
            scores = jnp.where(((a ^ b) & (GROUP - 1)) == 0, scores, -1e30)
            weights = jnp.exp(scores - jnp.max(scores, axis=1, keepdims=True))
            p = weights / jnp.sum(weights, axis=1, keepdims=True)
            probs_t[PART * half + h] = p
            acc0[:, cols] += dot(p.astype(BF16), v[:, cols] * keep)
            return carry

        lax.fori_loop(0, PART, head, 0, unroll=4)

    def backward(half):
        q, k, v, dm = qt.at[half], kt.at[half], vt.at[half], dt.at[half]
        for out in (acc0, acc1, acc2):
            out[...] = jnp.zeros_like(out)

        def head(h, carry):
            cols, keep = window(h)
            p = probs_t[PART * half + h]
            dm_h = dm[:, cols] * keep
            acc2[:, cols] += dot(p.astype(BF16), dm_h, ((0,), (0,)))
            dp = dot(dm_h, v[:, cols], ((1,), (1,)))
            dsc = (p * (dp - jnp.sum(dp * p, axis=1, keepdims=True))).astype(BF16)
            acc0[:, cols] += dot(dsc, k[:, cols] * keep)
            acc1[:, cols] += dot(dsc, q[:, cols] * keep, ((0,), (0,)))
            return carry

        lax.fori_loop(0, PART, head, 0, unroll=4)
        a = acc0[...] * SCALING
        b = pltpu.roll(acc1[...] * SCALING, 32, 1)
        c = pltpu.roll(acc2[...], 64, 1)

        def put(low, value):
            high = low + value.shape[1]
            gts[half, :, :, low:high] = value.reshape(FRAMES, GROUP, high - low).astype(BF16)

        put(0, a[:, 0:256])
        put(256, a[:, 256:PAD] + b[:, 0:128])
        put(384, b[:, 128:256])
        put(512, b[:, 256:PAD] + c[:, 0:128])
        put(640, c[:, 128:PAD])
        fields_back[half][0]()
        own[half].start()

    def forward_spatial(h, carry):
        scores = dot(qkvs[h], qkvs[HEADS + h], ((0,), (0,))) * SCALING
        weights = jnp.exp(scores - jnp.max(scores, axis=1, keepdims=True))
        p = weights / jnp.sum(weights, axis=1, keepdims=True)
        probs_s[h] = p
        rows = pl.ds(pl.multiple_of((h >> 1) * HEAD_DIM, 8), HEAD_DIM)
        mixs[h & 1, rows, :] = dot(qkvs[2 * HEADS + h], p.astype(BF16), ((1,), (1,)))
        return carry

    def backward_spatial(h, carry):
        p = probs_s[h]
        rows = pl.ds(pl.multiple_of((h >> 1) * HEAD_DIM, 8), HEAD_DIM)
        dm_h = dms[h & 1, rows, :].astype(BF16)
        dv = dot(dm_h, p.astype(BF16))
        dp = dot(dm_h, qkvs[2 * HEADS + h], ((0,), (0,)))
        dsc = (p * (dp - jnp.sum(dp * p, axis=1, keepdims=True))).astype(BF16)
        dq = dot(qkvs[HEADS + h], dsc, ((1,), (1,))) * SCALING
        dk = dot(qkvs[h], dsc) * SCALING
        gsb[h] = dq.astype(BF16)
        gsb[HEADS + h] = dk.astype(BF16)
        gsb[2 * HEADS + h] = dv.astype(BF16)
        return carry

    def rows_x(b):
        return [
            remote(
                wx.at[0, b, x], wx.at[0, b, x], wx_s.at[b, step], wx_r.at[b, step], at_x(step)
            )
            for step in (1, 2, 3)
        ]

    along_x = [rows_x(b) for b in (0, 1)]

    def rows_x_start(b):
        parts = [wz[i].astype(F32)[ROWS * b : ROWS * (b + 1)] for i in range(4)]
        wx[0, b, x] = jnp.concatenate(parts, axis=0).astype(BF16)
        for copy in along_x[b]:
            copy.start()

    to_partner = [
        remote(wx.at[0, b], wx.at[1, b], ww_s.at[b], ww_r.at[b], partner) for b in (0, 1)
    ]

    def rows_swap(b):
        for copy in along_x[b]:
            copy.wait_recv()
        to_partner[b].start()

    def rows_all(b):
        to_partner[b].wait_recv()
        for which in (0, 1):
            half = wx[which, b].astype(F32).reshape(HALF, D).astype(BF16)
            wmat[HALF * which : HALF * (which + 1), :] = half

    local[1].wait()
    lax.fori_loop(0, HEADS, forward_spatial, 0, unroll=4)

    def mixed_start(u, mixed, dims):
        m2[u, 0] = dot(selg[0], mixed, dims).astype(BF16)
        m2[u, 1] = dot(selg[1], mixed, dims).astype(BF16)
        copy = remote(m2.at[u, 1], m2.at[u, 2], p_s.at[u], p_r.at[u], partner)
        copy.start()
        return copy

    def flat(rows):
        return rows.astype(F32).reshape(PATCHES, D).astype(BF16)

    def along(u):
        return [
            remote(
                gbuf.at[u, (y + step) & 3], yrecv.at[u, step],
                y_s.at[u, step], y_r.at[u, step], at_y(step),
            )
            for step in (1, 2, 3)
        ]

    def reduce_y_start(u, cotangents, swap):
        share = dot(m2[u, 0], cotangents[0])
        swap.wait()
        share += dot(m2[u, 2], cotangents[1])
        gbuf[u] = (share * FACTOR).reshape(4, PAIR, D).astype(BF16)
        for copy in along(u):
            copy.start()

    def send_x(u, i):
        to = 2 * (u & 1) + i
        return to, remote(
            xbuf.at[u, i], xrecv.at[u, (x - to) & 3],
            x_s.at[u, i], x_r.at[u, (x - to) & 3], at(rep, zl * 8 + to * 2 + core),
        )

    def reduce_x_start(u):
        for copy in along(u):
            copy.wait()
        total = gbuf[u, y].astype(F32)
        for step in (1, 2, 3):
            total += yrecv[u, step].astype(F32)
        ysum[...] = total
        for i in (0, 1):
            rows = ysum[ROWS * i : ROWS * (i + 1), :]
            xbuf[u, i] = jnp.concatenate(
                [rows, jnp.zeros((BLOCK - ROWS, D), F32)], axis=0
            ).astype(BF16)
            to, copy = send_x(u, i)
            pl.when(x != to)(copy.start)

    def reduce_x_end(u):
        for i in (0, 1):
            to, copy = send_x(u, i)
            pl.when(x != to)(copy.wait_send)

    def here(u):
        return (x >> 1) == (u & 1)

    def reduce_z_start(u):
        b = u >> 1

        @pl.when(here(u))
        def _():
            total = xbuf[u, x & 1].astype(F32)
            for step in (1, 2, 3):
                arrived = xrecv.at[u, step]
                remote(arrived, arrived, x_s.at[u, 0], x_r.at[u, step], partner).wait_recv()
                total += xrecv[u, step].astype(F32)
            zbuf[b] = total.astype(BF16)
            pl.when(zl != y)(gather_z(b, 0).start)

    def gather_z(b, step):
        slot = lax.rem(zl - y + 4, 4) if step == 0 else step
        return remote(
            zbuf.at[b], zrecv.at[b, slot], z_s.at[b], z_r.at[b, slot],
            at(rep, y * 8 + lax.rem(me, 8)),
        )

    def spread_zh(b):
        return [
            remote(
                z2buf.at[b], z2recv.at[b, step], zz_s.at[b, step], zz_r.at[b, step], at_zh(step)
            )
            for step in (1, 2, 3)
        ]

    def reduce_zh_start(u):
        b = u >> 1

        @pl.when(here(u))
        def _stage():
            @pl.when(zl != y)
            def _():
                gather_z(b, 0).wait_send()

            @pl.when(zl == y)
            def _():
                total = zbuf[b].astype(F32)
                for step in (1, 2, 3):
                    gather_z(b, step).wait_recv()
                    total += zrecv[b, step].astype(F32)
                z2buf[b] = total.astype(BF16)
                for copy in spread_zh(b):
                    copy.start()

    def spread_y(b):
        return [
            remote(res.at[b], res.at[b], f_s.at[b, step], f_r.at[b], at_y(step))
            for step in (1, 2, 3)
        ]

    def spread_start(u):
        b = u >> 1

        @pl.when(here(u))
        def _stage():
            @pl.when(zl == y)
            def _():
                total = z2buf[b].astype(F32)
                for step, copy in zip((1, 2, 3), spread_zh(b), strict=True):
                    copy.wait()
                    total += z2recv[b, step].astype(F32)
                res[b] = total.astype(BF16)
                for copy in spread_y(b):
                    copy.start()

    def spread_end(u):
        b = u >> 1

        @pl.when(here(u))
        def _stage():
            @pl.when(zl == y)
            def _():
                for copy in spread_y(b):
                    copy.wait_send()

            @pl.when(zl != y)
            def _():
                spread_y(b)[0].wait_recv()

    swap_s = [mixed_start(half, mixs[half].astype(BF16), ((1,), (0,))) for half in (0, 1)]
    for copy in along_y:
        copy.wait_recv()
    rows_x_start(1)
    own = [
        pltpu.make_async_copy(gts.at[0, me], gtr.at[0, me], lsem.at[4]),
        pltpu.make_async_copy(gts.at[1, me], gtr.at[1, me], lsem.at[6]),
        pltpu.make_async_copy(gsb, gs_ref, lsem.at[7]),
        pltpu.make_async_copy(gto, gt_ref, lsem.at[8]),
        pltpu.make_async_copy(res, gw_ref, lsem.at[11]),
    ]
    og_copy.wait()
    ogt[0] = flat(og2[0])
    ogt[1] = flat(og2[1])
    for half in (0, 1):
        reduce_y_start(half, (ogt[0], ogt[1]), swap_s[half])
    rows_swap(1)

    def forward_half(half):
        own_fields[half].wait()
        fields_out[half][1]()
        split(half)
        forward(half)
        return mixed_start(2 + half, acc0[...].astype(BF16), ((1,), (1,)))

    for half in (0, 1):
        reduce_x_start(half)
    swap_t = forward_half(0)
    for half in (0, 1):
        reduce_z_start(half)
    rows_all(1)
    rows_x_start(0)

    local[4].wait()
    cotangent_out[1]()
    ogr_copy = remote(ogr.at[0], ogr.at[1], og_s.at[1], og_r.at[1], partner)
    ogr_copy.start()
    ogt[0] = flat(ogr[0])
    dah = dot(ogt[0], wmat[...], ((1,), (1,))).astype(BF16)
    for half in (0, 1):
        dt[half] = dot(dah, selw[half]).astype(BF16)
    ogr_copy.wait()
    ogt[1] = flat(ogr[1])
    reduce_y_start(2, (ogt[0], ogt[1]), swap_t)
    for half in (0, 1):
        reduce_zh_start(half)
    rows_swap(0)
    backward(0)
    reduce_x_start(2)

    swap_t = forward_half(1)
    reduce_y_start(3, (ogt[0], ogt[1]), swap_t)
    reduce_z_start(2)
    backward(1)
    reduce_x_start(3)
    reduce_z_start(3)
    for half in (0, 1):
        spread_start(half)
    reduce_zh_start(2)

    def turn_back(half):
        own[half].wait()
        fields_back[half][1]()
        for first in range(0, FIELDS, 128):
            part = gtr[half, :, :, first : first + 128].astype(F32)
            turn[first : first + 128, :] = part.reshape(PATCHES, 128).T
        for row, field in units(half):
            gto[field] = turn[row : row + HEAD_DIM, :].astype(BF16)
    reduce_zh_start(3)
    turn_back(0)
    spread_start(2)

    rows_all(0)
    dah = dot(wmat[...], flat(og2[0]), ((1,), (1,))).astype(BF16)
    for half in (0, 1):
        dms[half] = dot(selw[half], dah, ((0,), (0,)))
    lax.fori_loop(0, HEADS, backward_spatial, 0, unroll=2)
    own[2].start()

    spread_start(3)
    turn_back(1)
    own[3].start()
    for u in range(4):
        spread_end(u)
    own[4].start()

    for copy in along_y + along_x[0] + along_x[1] + to_partner:
        copy.wait_send()

    @pl.when(zl == y)
    def _():
        for copy in along_z:
            copy.wait_send()

    for u in range(4):
        reduce_x_end(u)
    cotangent_out[2]()
    for half in (0, 1):
        fields_out[half][2]()
        fields_back[half][2]()
    for copy in own[2:]:
        copy.wait()


def finish(gs_ref, gt_ref, rows_ref, gs_out, gt_out, rows_out, fields, rows, sems):
    load = [pltpu.make_async_copy(rows_ref, rows, sems.at[0])]
    store = []
    for i, (src, dst) in enumerate(((gs_ref, gs_out), (gt_ref, gt_out))):
        for w in range(3):
            part, k = pl.ds(HEADS * w, HEADS), 3 * i + w
            load.append(pltpu.make_async_copy(src.at[part], fields.at[k], sems.at[1 + k]))
            store.append(pltpu.make_async_copy(fields.at[k], dst.at[part], sems.at[7 + k]))
    for copy in load:
        copy.start()
    load[0].wait()
    both = [rows[b].astype(F32)[0:ROWS] for b in (0, 1)]
    rows_out[...] = jnp.stack(both, axis=1).astype(BF16)
    for arrived, copy in zip(load[1:], store, strict=True):
        arrived.wait()
        copy.start()
    for copy in store:
        copy.wait()


def per_device(qkv_spatial, qkv_temporal, out_grad, out_proj):
    def vmem(*shape, dtype=BF16):
        return pltpu.VMEM(shape, dtype)

    dma = pltpu.SemaphoreType.DMA
    scratch = [
        vmem(3 * HEADS, HEAD_DIM, PATCHES),
        vmem(3 * HEADS, HEAD_DIM, PATCHES),
        vmem(2, FRAMES, GROUP, D),
        vmem(3 * HEADS, HEAD_DIM, PATCHES),
        vmem(2, FRAMES, GROUP, FIELDS),
        vmem(2, FRAMES, GROUP, FIELDS),
        vmem(2, FRAMES, GROUP, D),
        vmem(2, PATCHES, D),
        vmem(2, FRAMES, GROUP, FIELDS),
        vmem(2, FRAMES, GROUP, FIELDS),
        vmem(3 * HEADS, HEAD_DIM, PATCHES),
        vmem(ROWS, 2, D),
        vmem(PAIR, D),
        vmem(4, PAIR, D),
        vmem(2, 2, 4, QUAD, D),
        vmem(INNER, D),
        vmem(2, INNER, PAD),
        vmem(2, 4 * PAIR, PAD),
        vmem(4, 3, 4 * PAIR, PATCHES),
        vmem(4, 4, PAIR, D),
        vmem(4, 4, PAIR, D),
        vmem(PAIR, D, dtype=F32),
        vmem(4, 2, BLOCK, D),
        vmem(4, 4, BLOCK, D),
        vmem(2, BLOCK, D),
        vmem(2, 4, BLOCK, D),
        vmem(2, BLOCK, D),
        vmem(2, 4, BLOCK, D),
        vmem(2, BLOCK, D),
        *[vmem(2, PATCHES, PAD) for _ in range(4)],
        vmem(HEADS, PATCHES, PATCHES, dtype=F32),
        vmem(HEADS, PATCHES, PATCHES, dtype=F32),
        *[vmem(PATCHES, PAD, dtype=F32) for _ in range(3)],
        *[vmem(2, PAD, PATCHES, dtype=F32) for _ in range(2)],
        vmem(FIELDS, PATCHES, dtype=F32),
        dma((12,)),
        dma((3,)), dma((1,)),
        dma((4,)), dma((4,)),
        dma((2, 4)), dma((2, 4)),
        dma((2,)), dma((2,)),
        dma((2,)), dma((2,)),
        dma((2, SEQ)), dma((2, SEQ)),
        dma((SEQ,)), dma((SEQ,)),
        dma((2, SEQ)), dma((2, SEQ)),
        dma((4,)), dma((4,)),
        dma((4, 4)), dma((4, 4)),
        dma((4, 2)), dma((4, 4)),
        dma((2,)), dma((2, 4)),
        dma((2, 4)), dma((2, 4)),
        dma((2, 4)), dma((2,)),
    ]
    hbm = pl.BlockSpec(memory_space=pl.ANY)
    spatial, temporal, rows = pl.pallas_call(
        kernel,
        name="attention_backward",
        out_shape=[
            jax.ShapeDtypeStruct((3 * HEADS, HEAD_DIM, PATCHES), BF16),
            jax.ShapeDtypeStruct((3 * HEADS, HEAD_DIM, PATCHES), BF16),
            jax.ShapeDtypeStruct((2, BLOCK, D), BF16),
        ],
        in_specs=[hbm] * 4,
        out_specs=[hbm] * 3,
        scratch_shapes=scratch,
        compiler_params=pltpu.CompilerParams(
            collective_id=0, has_side_effects=True, vmem_limit_bytes=56 * 2**20
        ),
    )(
        qkv_spatial.T.reshape(3 * HEADS, HEAD_DIM, PATCHES),
        qkv_temporal.T.reshape(3 * HEADS, HEAD_DIM, PATCHES),
        out_grad.reshape(FRAMES, GROUP, D),
        out_proj,
    )
    spatial, temporal, rows = pl.pallas_call(
        finish,
        name="finish",
        out_shape=[
            jax.ShapeDtypeStruct((3 * HEADS, HEAD_DIM, PATCHES), BF16),
            jax.ShapeDtypeStruct((3 * HEADS, HEAD_DIM, PATCHES), BF16),
            jax.ShapeDtypeStruct((ROWS, 2, D), BF16),
        ],
        in_specs=[hbm] * 3,
        out_specs=[hbm, hbm, pl.BlockSpec(memory_space=pltpu.VMEM)],
        scratch_shapes=[vmem(6, HEADS, HEAD_DIM, PATCHES), vmem(2, BLOCK, D), dma((13,))],
        compiler_params=pltpu.CompilerParams(vmem_limit_bytes=56 * 2**20),
    )(spatial, temporal, rows)
    return spatial.reshape(WIDTH, PATCHES).T, temporal.reshape(WIDTH, PATCHES).T, rows


def solution(mesh):
    placed = (
        P(("rep", "seq"), None),
        P(("rep", "seq"), None),
        P(("rep", "seq"), None),
        P("seq", None, None),
    )
    return jax.shard_map(
        per_device,
        mesh=mesh,
        in_specs=placed,
        out_specs=(P(("rep", "seq"), None), P(("rep", "seq"), None), P("seq", None, None)),
        check_vma=False,
    )
```

```python
import functools

import jax
import jax.numpy as jnp
from jax import lax
from jax.experimental import pallas as pl
from jax.experimental.pallas import tpu as pltpu
from jax.sharding import PartitionSpec as P

HEADS, HEAD_DIM, PATCHES, FRAMES = 8, 72, 256, 32
INNER, WIDTH, D = 576, 1728, 1152
PART = 4
PAD = 384
FIELDS = 896
GROUP = 8
ROWS = 18
BLOCK = 24
PAIR = 40
QUAD = 4 * ROWS
HALF = 4 * QUAD
SEQ, TOKENS = 32, 131072
SCALING = HEAD_DIM**-0.5
FACTOR = float(TOKENS) ** -0.5
F32, BF16 = jnp.float32, jnp.bfloat16


def dot(left, right, dims=((1,), (0,))):
    return lax.dot_general(left, right, (dims, ((), ())), preferred_element_type=F32)


def kernel(
    qkvs_ref, qkvt_ref, og_ref, w_ref,
    gs_ref, gt_ref, gw_ref,
    qkvs, gsb, og2, qtin, qts, qtr, ogr, ogt, gts, gtr, gto, wraw, wown, wz, wx, wmat, selw, selg, m2,
    gbuf, yrecv, ysum, xbuf, xrecv, zbuf, zrecv, z2buf, z2recv, res,
    qt, kt, vt, dt, probs_s, probs_t, acc0, acc1, acc2, mixs, dms, turn,
    lsem, wz_s, wz_r, wy_s, wy_r, wx_s, wx_r, ww_s, ww_r, og_s, og_r, a_s, a_r, b_s, b_r, d_s, d_r,
    p_s, p_r, y_s, y_r, x_s, x_r, z_s, z_r, zz_s, zz_r, f_s, f_r,
):
    rep, me = lax.axis_index("rep"), lax.axis_index("seq")
    zh, y = rep // 4, lax.rem(rep, 4)
    zl, x, core = me // 8, lax.rem(me // 2, 4), lax.rem(me, 2)
    z = 4 * zh + zl

    def at(rep_to, seq_to):
        return {"device_id": (rep_to, seq_to), "device_id_type": pl.DeviceIdType.MESH}

    def at_z(step):
        to = lax.rem(z + step + 16, 16)
        return at((to // 4) * 4 + y, lax.rem(to, 4) * 8 + lax.rem(me, 8))

    def at_y(step):
        return at(zh * 4 + lax.rem(y + step, 4), me)

    def at_zh(step):
        return at(lax.rem(zh + step, 4) * 4 + y, me)

    def at_x(step):
        return at(rep, zl * 8 + lax.rem(x + step, 4) * 2 + core)

    partner = at(rep, me + 1 - 2 * core)

    def remote(src, dst, send, recv, target):
        return pltpu.make_async_remote_copy(
            src_ref=src, dst_ref=dst, send_sem=send, recv_sem=recv, **target
        )

    barrier = pltpu.get_barrier_semaphore()

    def greet(k, carry):
        pl.semaphore_signal(barrier, inc=1, **at(rep, lax.rem(me + k, SEQ)))
        return carry

    lax.fori_loop(1, SEQ, greet, 0)
    for step in (-1, -2, 1):
        pl.semaphore_signal(barrier, inc=1, **at_z(step))
    for step in (1, 2, 3):
        pl.semaphore_signal(barrier, inc=1, **at_y(step))
        pl.semaphore_signal(barrier, inc=1, **at_zh(step))

    local = [
        pltpu.make_async_copy(w_ref, wraw, lsem.at[0]),
        pltpu.make_async_copy(qkvs_ref, qkvs, lsem.at[1]),
        pltpu.make_async_copy(og_ref, og2.at[0], lsem.at[2]),
        pltpu.make_async_copy(qkvt_ref, qtin, lsem.at[3]),
        pltpu.make_async_copy(og_ref.at[me], ogr.at[0, me], lsem.at[5]),
    ]
    for copy in local:
        copy.start()
    local[0].wait()
    own_rows = wraw[...].astype(F32)
    rest = jnp.zeros((PAIR - 2 * ROWS, D), F32)
    own_rows = jnp.concatenate([own_rows[:, 0, :], own_rows[:, 1, :], rest], axis=0)
    wown[...] = own_rows.astype(BF16)

    @pl.when(zl == y)
    def _():
        wz[y] = wown[...]

    def units(half):
        return [
            (HEAD_DIM * (PART * w + i), HEADS * w + 2 * i + half) for w in range(3) for i in range(PART)
        ]

    local[3].wait()
    turn[3 * PART * HEAD_DIM :, :] = jnp.zeros((FIELDS - 3 * PART * HEAD_DIM, PATCHES), F32)
    own_fields = []

    def turn_fields(half):
        for row, field in units(half):
            turn[row : row + HEAD_DIM, :] = qtin[field].astype(F32)
        for first in range(0, FIELDS, 128):
            part = turn[first : first + 128, :].T.reshape(FRAMES, GROUP, 128)
            qts[half, :, :, first : first + 128] = part.astype(BF16)
        copy = pltpu.make_async_copy(qts.at[half, me], qtr.at[half, me], lsem.at[9 + half])
        copy.start()
        own_fields.append(copy)

    turn_fields(0)

    pl.semaphore_wait(barrier, 31 + 9)

    along_z = [
        remote(wown, wz.at[y], wz_s.at[i], wz_r.at[0], at_z(step))
        for i, step in enumerate((1, 2, -1))
    ]
    along_y = [
        remote(wz.at[y], wz.at[y], wy_s.at[step], wy_r.at[step], at_y(step))
        for step in (1, 2, 3)
    ]

    @pl.when(zl == y)
    def _():
        for copy in along_z + along_y:
            copy.start()

    def exchange(src, dst, send, recv):
        def copy(k):
            to = lax.rem(me + k, SEQ)
            return remote(src.at[to], dst.at[me], send.at[k], recv.at[k], at(rep, to))

        def start(k, carry):
            copy(k).start()
            return carry

        def landed(k, carry):
            copy(k).wait_recv()
            return carry

        def sent(k, carry):
            copy(k).wait_send()
            return carry

        return (
            lambda: lax.fori_loop(1, SEQ, start, 0),
            lambda: lax.fori_loop(1, SEQ, landed, 0),
            lambda: lax.fori_loop(1, SEQ, sent, 0),
        )

    fields_out = [
        exchange(qts.at[half], qtr.at[half], a_s.at[half], a_r.at[half]) for half in (0, 1)
    ]
    cotangent_out = exchange(og_ref, ogr.at[0], b_s, b_r)
    fields_back = [
        exchange(gts.at[half], gtr.at[half], d_s.at[half], d_r.at[half]) for half in (0, 1)
    ]
    fields_out[0][0]()
    cotangent_out[0]()
    turn_fields(1)
    fields_out[1][0]()

    @pl.when(zl != y)
    def _():
        along_z[0].wait_recv()
        for copy in along_y:
            copy.start()

    og_copy = remote(og2.at[0], og2.at[1], og_s.at[0], og_r.at[0], partner)
    local[2].wait()
    og_copy.start()

    r = lax.broadcasted_iota(jnp.int32, (HALF, 1), 0)
    block = (r * 3641) >> 16
    high, low, j = block >> 2, block & 3, r - ROWS * block
    n = lax.broadcasted_iota(jnp.int32, (HALF, PAD), 1)
    for which in (0, 1):
        parity = core if which == 0 else 1 - core
        own = ROWS * (8 * low + 2 * high + parity) + j
        head = (own * 911) >> 16
        column = HEAD_DIM * (head >> 1) + own - HEAD_DIM * head
        for half in (0, 1):
            hit = (n == column) & ((head & 1) == half)
            selw[half, HALF * which : HALF * (which + 1), :] = jnp.where(hit, 1.0, 0.0).astype(BF16)
    r = lax.broadcasted_iota(jnp.int32, (4 * PAIR, 1), 0)
    n = lax.broadcasted_iota(jnp.int32, (4 * PAIR, PAD), 1)
    high = (r * 1639) >> 16
    low = jnp.where(r - PAIR * high >= ROWS, 1, 0)
    j = r - PAIR * high - ROWS * low
    for which in (0, 1):
        parity = core if which == 0 else 1 - core
        hit = (n == HEAD_DIM * high + ROWS * (2 * low + parity) + j) & (j < ROWS)
        selg[which] = jnp.where(hit, 1.0, 0.0).astype(BF16)
    mixs[...] = jnp.zeros_like(mixs)

    def split(half):
        fields = qtr[half].astype(F32).reshape(PATCHES, FIELDS)
        qt[half] = fields[:, 0:PAD].astype(BF16)
        kt[half] = pltpu.roll(fields[:, 256:640], PAD - 32, 1).astype(BF16)
        vt[half] = pltpu.roll(fields[:, 512:FIELDS], PAD - 64, 1).astype(BF16)

    def window(h):
        first = (HEAD_DIM * h) // 128
        lane = lax.broadcasted_iota(jnp.int32, (1, 256), 1) + first * 128 - HEAD_DIM * h
        keep = jnp.where((lane >= 0) & (lane < HEAD_DIM), 1.0, 0.0).astype(BF16)
        return pl.ds(pl.multiple_of(first * 128, 128), 256), keep

    def forward(half):
        q, k, v = qt.at[half], kt.at[half], vt.at[half]
        acc0[...] = jnp.zeros_like(acc0)

        def head(h, carry):
            cols, keep = window(h)
            scores = dot(q[:, cols], k[:, cols] * keep, ((1,), (1,))) * SCALING
            a = lax.broadcasted_iota(jnp.int32, scores.shape, 0)
            b = lax.broadcasted_iota(jnp.int32, scores.shape, 1)
            scores = jnp.where(((a ^ b) & (GROUP - 1)) == 0, scores, -1e30)
            weights = jnp.exp(scores - jnp.max(scores, axis=1, keepdims=True))
            p = weights / jnp.sum(weights, axis=1, keepdims=True)
            probs_t[PART * half + h] = p
            acc0[:, cols] += dot(p.astype(BF16), v[:, cols] * keep)
            return carry

        lax.fori_loop(0, PART, head, 0, unroll=4)

    def backward(half):
        q, k, v, dm = qt.at[half], kt.at[half], vt.at[half], dt.at[half]
        for out in (acc0, acc1, acc2):
            out[...] = jnp.zeros_like(out)

        def head(h, carry):
            cols, keep = window(h)
            p = probs_t[PART * half + h]
            dm_h = dm[:, cols] * keep
            acc2[:, cols] += dot(p.astype(BF16), dm_h, ((0,), (0,)))
            dp = dot(dm_h, v[:, cols], ((1,), (1,)))
            dsc = (p * (dp - jnp.sum(dp * p, axis=1, keepdims=True))).astype(BF16)
            acc0[:, cols] += dot(dsc, k[:, cols] * keep)
            acc1[:, cols] += dot(dsc, q[:, cols] * keep, ((0,), (0,)))
            return carry

        lax.fori_loop(0, PART, head, 0, unroll=4)
        a = acc0[...] * SCALING
        b = pltpu.roll(acc1[...] * SCALING, 32, 1)
        c = pltpu.roll(acc2[...], 64, 1)

        def put(low, value):
            high = low + value.shape[1]
            gts[half, :, :, low:high] = value.reshape(FRAMES, GROUP, high - low).astype(BF16)

        put(0, a[:, 0:256])
        put(256, a[:, 256:PAD] + b[:, 0:128])
        put(384, b[:, 128:256])
        put(512, b[:, 256:PAD] + c[:, 0:128])
        put(640, c[:, 128:PAD])
        fields_back[half][0]()
        own[half].start()

    def forward_spatial(h, carry):
        scores = dot(qkvs[h], qkvs[HEADS + h], ((0,), (0,))) * SCALING
        weights = jnp.exp(scores - jnp.max(scores, axis=1, keepdims=True))
        p = weights / jnp.sum(weights, axis=1, keepdims=True)
        probs_s[h] = p
        rows = pl.ds(pl.multiple_of((h >> 1) * HEAD_DIM, 8), HEAD_DIM)
        mixs[h & 1, rows, :] = dot(qkvs[2 * HEADS + h], p.astype(BF16), ((1,), (1,)))
        return carry

    def backward_spatial(h, carry):
        p = probs_s[h]
        rows = pl.ds(pl.multiple_of((h >> 1) * HEAD_DIM, 8), HEAD_DIM)
        dm_h = dms[h & 1, rows, :].astype(BF16)
        dv = dot(dm_h, p.astype(BF16))
        dp = dot(dm_h, qkvs[2 * HEADS + h], ((0,), (0,)))
        dsc = (p * (dp - jnp.sum(dp * p, axis=1, keepdims=True))).astype(BF16)
        dq = dot(qkvs[HEADS + h], dsc, ((1,), (1,))) * SCALING
        dk = dot(qkvs[h], dsc) * SCALING
        gsb[h] = dq.astype(BF16)
        gsb[HEADS + h] = dk.astype(BF16)
        gsb[2 * HEADS + h] = dv.astype(BF16)
        return carry

    def rows_x(b):
        return [
            remote(
                wx.at[0, b, x], wx.at[0, b, x], wx_s.at[b, step], wx_r.at[b, step], at_x(step)
            )
            for step in (1, 2, 3)
        ]

    along_x = [rows_x(b) for b in (0, 1)]

    def rows_x_start(b):
        parts = [wz[i].astype(F32)[ROWS * b : ROWS * (b + 1)] for i in range(4)]
        wx[0, b, x] = jnp.concatenate(parts, axis=0).astype(BF16)
        for copy in along_x[b]:
            copy.start()

    to_partner = [
        remote(wx.at[0, b], wx.at[1, b], ww_s.at[b], ww_r.at[b], partner) for b in (0, 1)
    ]

    def rows_swap(b):
        for copy in along_x[b]:
            copy.wait_recv()
        to_partner[b].start()

    def rows_all(b):
        to_partner[b].wait_recv()
        for which in (0, 1):
            half = wx[which, b].astype(F32).reshape(HALF, D).astype(BF16)
            wmat[HALF * which : HALF * (which + 1), :] = half

    local[1].wait()
    lax.fori_loop(0, HEADS, forward_spatial, 0, unroll=4)

    def mixed_start(u, mixed, dims):
        m2[u, 0] = dot(selg[0], mixed, dims).astype(BF16)
        m2[u, 1] = dot(selg[1], mixed, dims).astype(BF16)
        copy = remote(m2.at[u, 1], m2.at[u, 2], p_s.at[u], p_r.at[u], partner)
        copy.start()
        return copy

    def flat(rows):
        return rows.astype(F32).reshape(PATCHES, D).astype(BF16)

    def along(u):
        return [
            remote(
                gbuf.at[u, (y + step) & 3], yrecv.at[u, step],
                y_s.at[u, step], y_r.at[u, step], at_y(step),
            )
            for step in (1, 2, 3)
        ]

    def reduce_y_start(u, cotangents, swap):
        share = dot(m2[u, 0], cotangents[0])
        swap.wait()
        share += dot(m2[u, 2], cotangents[1])
        gbuf[u] = (share * FACTOR).reshape(4, PAIR, D).astype(BF16)
        for copy in along(u):
            copy.start()

    def send_x(u, i):
        to = 2 * (u & 1) + i
        return to, remote(
            xbuf.at[u, i], xrecv.at[u, (x - to) & 3],
            x_s.at[u, i], x_r.at[u, (x - to) & 3], at(rep, zl * 8 + to * 2 + core),
        )

    def reduce_x_start(u):
        for copy in along(u):
            copy.wait()
        total = gbuf[u, y].astype(F32)
        for step in (1, 2, 3):
            total += yrecv[u, step].astype(F32)
        ysum[...] = total
        for i in (0, 1):
            rows = ysum[ROWS * i : ROWS * (i + 1), :]
            xbuf[u, i] = jnp.concatenate(
                [rows, jnp.zeros((BLOCK - ROWS, D), F32)], axis=0
            ).astype(BF16)
            to, copy = send_x(u, i)
            pl.when(x != to)(copy.start)

    def reduce_x_end(u):
        for i in (0, 1):
            to, copy = send_x(u, i)
            pl.when(x != to)(copy.wait_send)

    def here(u):
        return (x >> 1) == (u & 1)

    def reduce_z_start(u):
        b = u >> 1

        @pl.when(here(u))
        def _():
            total = xbuf[u, x & 1].astype(F32)
            for step in (1, 2, 3):
                arrived = xrecv.at[u, step]
                remote(arrived, arrived, x_s.at[u, 0], x_r.at[u, step], partner).wait_recv()
                total += xrecv[u, step].astype(F32)
            zbuf[b] = total.astype(BF16)
            pl.when(zl != y)(gather_z(b, 0).start)

    def gather_z(b, step):
        slot = lax.rem(zl - y + 4, 4) if step == 0 else step
        return remote(
            zbuf.at[b], zrecv.at[b, slot], z_s.at[b], z_r.at[b, slot],
            at(rep, y * 8 + lax.rem(me, 8)),
        )

    def spread_zh(b):
        return [
            remote(
                z2buf.at[b], z2recv.at[b, step], zz_s.at[b, step], zz_r.at[b, step], at_zh(step)
            )
            for step in (1, 2, 3)
        ]

    def reduce_zh_start(u):
        b = u >> 1

        @pl.when(here(u))
        def _stage():
            @pl.when(zl != y)
            def _():
                gather_z(b, 0).wait_send()

            @pl.when(zl == y)
            def _():
                total = zbuf[b].astype(F32)
                for step in (1, 2, 3):
                    gather_z(b, step).wait_recv()
                    total += zrecv[b, step].astype(F32)
                z2buf[b] = total.astype(BF16)
                for copy in spread_zh(b):
                    copy.start()

    def spread_y(b):
        return [
            remote(res.at[b], res.at[b], f_s.at[b, step], f_r.at[b], at_y(step))
            for step in (1, 2, 3)
        ]

    def spread_start(u):
        b = u >> 1

        @pl.when(here(u))
        def _stage():
            @pl.when(zl == y)
            def _():
                total = z2buf[b].astype(F32)
                for step, copy in zip((1, 2, 3), spread_zh(b), strict=True):
                    copy.wait()
                    total += z2recv[b, step].astype(F32)
                res[b] = total.astype(BF16)
                for copy in spread_y(b):
                    copy.start()

    def spread_end(u):
        b = u >> 1

        @pl.when(here(u))
        def _stage():
            @pl.when(zl == y)
            def _():
                for copy in spread_y(b):
                    copy.wait_send()

            @pl.when(zl != y)
            def _():
                spread_y(b)[0].wait_recv()

    swap_s = [mixed_start(half, mixs[half].astype(BF16), ((1,), (0,))) for half in (0, 1)]
    for copy in along_y:
        copy.wait_recv()
    rows_x_start(1)
    own = [
        pltpu.make_async_copy(gts.at[0, me], gtr.at[0, me], lsem.at[4]),
        pltpu.make_async_copy(gts.at[1, me], gtr.at[1, me], lsem.at[6]),
        pltpu.make_async_copy(gsb, gs_ref, lsem.at[7]),
        pltpu.make_async_copy(gto, gt_ref, lsem.at[8]),
        pltpu.make_async_copy(res, gw_ref, lsem.at[11]),
    ]
    og_copy.wait()
    ogt[0] = flat(og2[0])
    ogt[1] = flat(og2[1])
    for half in (0, 1):
        reduce_y_start(half, (ogt[0], ogt[1]), swap_s[half])
    rows_swap(1)

    def forward_half(half):
        own_fields[half].wait()
        fields_out[half][1]()
        split(half)
        forward(half)
        return mixed_start(2 + half, acc0[...].astype(BF16), ((1,), (1,)))

    for half in (0, 1):
        reduce_x_start(half)
    swap_t = forward_half(0)
    for half in (0, 1):
        reduce_z_start(half)
    rows_all(1)
    rows_x_start(0)

    local[4].wait()
    cotangent_out[1]()
    ogr_copy = remote(ogr.at[0], ogr.at[1], og_s.at[1], og_r.at[1], partner)
    ogr_copy.start()
    ogt[0] = flat(ogr[0])
    dah = dot(ogt[0], wmat[...], ((1,), (1,))).astype(BF16)
    for half in (0, 1):
        dt[half] = dot(dah, selw[half]).astype(BF16)
    ogr_copy.wait()
    ogt[1] = flat(ogr[1])
    reduce_y_start(2, (ogt[0], ogt[1]), swap_t)
    for half in (0, 1):
        reduce_zh_start(half)
    rows_swap(0)
    backward(0)
    reduce_x_start(2)

    swap_t = forward_half(1)
    reduce_y_start(3, (ogt[0], ogt[1]), swap_t)
    reduce_z_start(2)
    backward(1)
    reduce_x_start(3)
    reduce_z_start(3)
    for half in (0, 1):
        spread_start(half)
    reduce_zh_start(2)

    def turn_back(half):
        own[half].wait()
        fields_back[half][1]()
        for first in range(0, FIELDS, 128):
            part = gtr[half, :, :, first : first + 128].astype(F32)
            turn[first : first + 128, :] = part.reshape(PATCHES, 128).T
        for row, field in units(half):
            gto[field] = turn[row : row + HEAD_DIM, :].astype(BF16)
    reduce_zh_start(3)
    turn_back(0)

    rows_all(0)
    dah = dot(wmat[...], flat(og2[0]), ((1,), (1,))).astype(BF16)
    for half in (0, 1):
        dms[half] = dot(selw[half], dah, ((0,), (0,)))
    lax.fori_loop(0, HEADS, backward_spatial, 0, unroll=2)
    own[2].start()

    spread_start(2)
    spread_start(3)
    turn_back(1)
    own[3].start()
    for u in range(4):
        spread_end(u)
    own[4].start()

    for copy in along_y + along_x[0] + along_x[1] + to_partner:
        copy.wait_send()

    @pl.when(zl == y)
    def _():
        for copy in along_z:
            copy.wait_send()

    for u in range(4):
        reduce_x_end(u)
    cotangent_out[2]()
    for half in (0, 1):
        fields_out[half][2]()
        fields_back[half][2]()
    for copy in own[2:]:
        copy.wait()


def finish(gs_ref, gt_ref, rows_ref, gs_out, gt_out, rows_out, fields, rows, sems):
    load = [pltpu.make_async_copy(rows_ref, rows, sems.at[0])]
    store = []
    for i, (src, dst) in enumerate(((gs_ref, gs_out), (gt_ref, gt_out))):
        for w in range(3):
            part, k = pl.ds(HEADS * w, HEADS), 3 * i + w
            load.append(pltpu.make_async_copy(src.at[part], fields.at[k], sems.at[1 + k]))
            store.append(pltpu.make_async_copy(fields.at[k], dst.at[part], sems.at[7 + k]))
    for copy in load:
        copy.start()
    load[0].wait()
    both = [rows[b].astype(F32)[0:ROWS] for b in (0, 1)]
    rows_out[...] = jnp.stack(both, axis=1).astype(BF16)
    for arrived, copy in zip(load[1:], store, strict=True):
        arrived.wait()
        copy.start()
    for copy in store:
        copy.wait()


def per_device(qkv_spatial, qkv_temporal, out_grad, out_proj):
    def vmem(*shape, dtype=BF16):
        return pltpu.VMEM(shape, dtype)

    dma = pltpu.SemaphoreType.DMA
    scratch = [
        vmem(3 * HEADS, HEAD_DIM, PATCHES),
        vmem(3 * HEADS, HEAD_DIM, PATCHES),
        vmem(2, FRAMES, GROUP, D),
        vmem(3 * HEADS, HEAD_DIM, PATCHES),
        vmem(2, FRAMES, GROUP, FIELDS),
        vmem(2, FRAMES, GROUP, FIELDS),
        vmem(2, FRAMES, GROUP, D),
        vmem(2, PATCHES, D),
        vmem(2, FRAMES, GROUP, FIELDS),
        vmem(2, FRAMES, GROUP, FIELDS),
        vmem(3 * HEADS, HEAD_DIM, PATCHES),
        vmem(ROWS, 2, D),
        vmem(PAIR, D),
        vmem(4, PAIR, D),
        vmem(2, 2, 4, QUAD, D),
        vmem(INNER, D),
        vmem(2, INNER, PAD),
        vmem(2, 4 * PAIR, PAD),
        vmem(4, 3, 4 * PAIR, PATCHES),
        vmem(4, 4, PAIR, D),
        vmem(4, 4, PAIR, D),
        vmem(PAIR, D, dtype=F32),
        vmem(4, 2, BLOCK, D),
        vmem(4, 4, BLOCK, D),
        vmem(2, BLOCK, D),
        vmem(2, 4, BLOCK, D),
        vmem(2, BLOCK, D),
        vmem(2, 4, BLOCK, D),
        vmem(2, BLOCK, D),
        *[vmem(2, PATCHES, PAD) for _ in range(4)],
        vmem(HEADS, PATCHES, PATCHES, dtype=F32),
        vmem(HEADS, PATCHES, PATCHES, dtype=F32),
        *[vmem(PATCHES, PAD, dtype=F32) for _ in range(3)],
        *[vmem(2, PAD, PATCHES, dtype=F32) for _ in range(2)],
        vmem(FIELDS, PATCHES, dtype=F32),
        dma((12,)),
        dma((3,)), dma((1,)),
        dma((4,)), dma((4,)),
        dma((2, 4)), dma((2, 4)),
        dma((2,)), dma((2,)),
        dma((2,)), dma((2,)),
        dma((2, SEQ)), dma((2, SEQ)),
        dma((SEQ,)), dma((SEQ,)),
        dma((2, SEQ)), dma((2, SEQ)),
        dma((4,)), dma((4,)),
        dma((4, 4)), dma((4, 4)),
        dma((4, 2)), dma((4, 4)),
        dma((2,)), dma((2, 4)),
        dma((2, 4)), dma((2, 4)),
        dma((2, 4)), dma((2,)),
    ]
    hbm = pl.BlockSpec(memory_space=pl.ANY)
    spatial, temporal, rows = pl.pallas_call(
        kernel,
        name="attention_backward",
        out_shape=[
            jax.ShapeDtypeStruct((3 * HEADS, HEAD_DIM, PATCHES), BF16),
            jax.ShapeDtypeStruct((3 * HEADS, HEAD_DIM, PATCHES), BF16),
            jax.ShapeDtypeStruct((2, BLOCK, D), BF16),
        ],
        in_specs=[hbm] * 4,
        out_specs=[hbm] * 3,
        scratch_shapes=scratch,
        compiler_params=pltpu.CompilerParams(
            collective_id=0, has_side_effects=True, vmem_limit_bytes=56 * 2**20
        ),
    )(
        qkv_spatial.T.reshape(3 * HEADS, HEAD_DIM, PATCHES),
        qkv_temporal.T.reshape(3 * HEADS, HEAD_DIM, PATCHES),
        out_grad.reshape(FRAMES, GROUP, D),
        out_proj,
    )
    spatial, temporal, rows = pl.pallas_call(
        finish,
        name="finish",
        out_shape=[
            jax.ShapeDtypeStruct((3 * HEADS, HEAD_DIM, PATCHES), BF16),
            jax.ShapeDtypeStruct((3 * HEADS, HEAD_DIM, PATCHES), BF16),
            jax.ShapeDtypeStruct((ROWS, 2, D), BF16),
        ],
        in_specs=[hbm] * 3,
        out_specs=[hbm, hbm, pl.BlockSpec(memory_space=pltpu.VMEM)],
        scratch_shapes=[vmem(6, HEADS, HEAD_DIM, PATCHES), vmem(2, BLOCK, D), dma((13,))],
        compiler_params=pltpu.CompilerParams(vmem_limit_bytes=56 * 2**20),
    )(spatial, temporal, rows)
    return spatial.reshape(WIDTH, PATCHES).T, temporal.reshape(WIDTH, PATCHES).T, rows


def solution(mesh):
    placed = (
        P(("rep", "seq"), None),
        P(("rep", "seq"), None),
        P(("rep", "seq"), None),
        P("seq", None, None),
    )
    return jax.shard_map(
        per_device,
        mesh=mesh,
        in_specs=placed,
        out_specs=(P(("rep", "seq"), None), P(("rep", "seq"), None), P("seq", None, None)),
        check_vma=False,
    )
```
